256 devices in a mesh: aux: 32 (over y, x, core), occ: 8 (over z).
Axes of the slice: x: 4, y: 4, z: 8, core: 2. Of those that a mesh axis runs over, the one named last changes fastest.
Arguments:
- integrals: bfloat16 [1024, 8, 128, 128], P('aux'), may hold values from -0.008361816 to 0.008361816
- screened_blocks: int32 [1024, 3], P('aux'), may hold values from 0 to 31, as said below
- coeff: bfloat16 [128, 24, 128], P('occ'), may hold values from -6 to 6
- support: int32 [8, 24], replicated, may hold values from 0 to 31, as said below
- metric: bfloat16 [4096, 4096], P('aux'), as said below
- block_order: int32 [32], replicated, may hold values from 0 to 31, each once
Outputs:
- exchange_panel: float32 [32, 128, 128], P('aux')
The draws below stay inside these ranges and needn't reach their ends.
Inputs may be any that keep to these rules, and one draw needn't show every extreme that they name: `screened_blocks`: column 0 and 1 are shell blocks below 32, column 2 an auxiliary block below 16. Among the 32 rows of one index of aux no mu block appears more than 2 times, and one mu block, the same for all indices, appears exactly 2 times in each. `support`: each row holds 24 different shell blocks. `metric`: Symmetric.
All inputs are finite; a program needn't handle non-finite values.
Results may differ from the reference program's by a relative error of at most 0.00087.
Values may be sent and summed in bfloat16 or wider, within the bound.
A program may use at most 128 MiB of HBM per device.

```python
import jax
import jax.numpy as jnp
from jax import lax

SHELL = 128
PANEL = 128
AUXB = 8
AUX_DEV = 128
NTRI = 32
ORB = 16
MB = 32
NSUP = 24
QB = 16
AUX = 4096
TRI = 1024
CAP = 2
N_AUX = 32
N_OCC = 8


def draw_screened_blocks(key, part):
    key = jax.random.fold_in(key, 11)
    hot_block = jax.random.randint(jax.random.fold_in(key, 1), (), 0, MB)

    def one_device(index):
        device_key = jax.random.fold_in(key, 100 + index)
        shuffled = jax.random.permutation(jax.random.fold_in(device_key, 1), MB * CAP)
        blocks_of = (shuffled // CAP).astype(jnp.int32)
        order = jnp.argsort((blocks_of != hot_block).astype(jnp.int32), stable=True)
        chosen = blocks_of[order][:NTRI]
        mixing = jax.random.permutation(jax.random.fold_in(device_key, 2), NTRI)
        mu_list = chosen[mixing]
        nu_list = jax.random.randint(jax.random.fold_in(device_key, 3), (NTRI,), 0, MB)
        q_list = jax.random.randint(jax.random.fold_in(device_key, 4), (NTRI,), 0, QB)
        return jnp.stack([mu_list, nu_list, q_list], axis=1).astype(jnp.int32)
    lists = jax.vmap(one_device)(jnp.arange(N_AUX, dtype=jnp.int32))
    return lists.reshape(TRI, 3)


def draw_support(key, part):
    key = jax.random.fold_in(key, 12)

    def one_panel(index):
        return jax.random.permutation(jax.random.fold_in(key, 50 + index), MB)[:NSUP].astype(jnp.int32)
    return jax.vmap(one_panel)(jnp.arange(N_OCC, dtype=jnp.int32))


def draw_metric(key, part):
    key = jax.random.fold_in(key, 13)
    diagonal = jnp.ones((AUX,), jnp.float32)
    raw = jax.random.normal(jax.random.fold_in(key, 2), (AUX, AUX), jnp.float32)
    offdiag = (raw + raw.T) * (0.35 / AUX ** 0.5)
    full = offdiag + jnp.diag(diagonal)
    return full.astype(jnp.bfloat16)


def block_levels(stream_key, extent, shards, smallest, high):
    factor_of, own = 1.0, jax.random.fold_in(stream_key, 6)
    for position, parts in shards:
        draws = jnp.exp(jax.random.uniform(jax.random.fold_in(own, position), (parts,), jnp.float32, smallest / len(shards), high / len(shards)))
        factor_of = factor_of * jnp.repeat(draws, extent[position] // parts).reshape([-1 if axis == position else 1 for axis in range(len(extent))])
    return factor_of


def scatter_about(key, extent, deviation, reach, cuts=(), kind=jnp.bfloat16):
    entries = jax.random.normal(key, extent, jnp.float32) * deviation
    if len(cuts) > 0:
        entries = block_levels(key, extent, cuts, -0.22, 0.18) * entries
    return jnp.clip(entries, min=-reach, max=reach).astype(kind)


def setup_inputs(seed: int = 0) -> dict:
    streams_of = jax.random.split(jax.random.key(seed), 7)
    integrals = scatter_about(streams_of[0], (TRI, AUXB, SHELL, SHELL), 0.0014, 0.008361816, ((0, 32),))
    screened_blocks = draw_screened_blocks(jax.random.fold_in(streams_of[6], 71), 0)
    coeff = scatter_about(streams_of[2], (PANEL, NSUP, SHELL), 1.0, 6.0, ((0, 8),))
    support = draw_support(jax.random.fold_in(streams_of[6], 71), 0)
    metric = draw_metric(jax.random.fold_in(streams_of[6], 71), 0)
    block_order = jax.random.permutation(streams_of[5], MB).astype(jnp.int32)
    return {"integrals": integrals, "screened_blocks": screened_blocks, "coeff": coeff, "support": support, "metric": metric, "block_order": block_order}


def dense_panel(coeff, support):
    onehot = (support[:, :, None] == jnp.arange(MB, dtype=jnp.int32)[None, None, :]).astype(jnp.float32)
    blocks = coeff.astype(jnp.float32).reshape(N_OCC, ORB, NSUP, SHELL)
    dense = jnp.einsum("osb,oisn->bnoi", onehot, blocks, precision=lax.Precision.HIGHEST)
    return dense.reshape(MB, SHELL, PANEL).astype(jnp.bfloat16)


def half_blocks(ints_dev, nu_list, panel_dense):
    coeff_nu = panel_dense[nu_list].astype(jnp.float32)
    return jnp.einsum("tamn,tni->taim", ints_dev.astype(jnp.float32), coeff_nu).astype(jnp.bfloat16)


def reference(integrals, screened_blocks, coeff, support, metric, block_order):
    panel_dense = dense_panel(coeff, support)
    ints_all = integrals.reshape(N_AUX, NTRI, AUXB, SHELL, SHELL)
    lists_all = screened_blocks.reshape(N_AUX, NTRI, 3)

    def fitted_input(carry, inputs):
        ints_dev, lists = inputs
        mu_list = lists[:, 0]
        transformed = half_blocks(ints_dev, lists[:, 1], panel_dense).astype(jnp.float32)
        coeff_mu = panel_dense[mu_list].astype(jnp.float32)
        term_parts = jnp.einsum("taim,tmj->taij", transformed, coeff_mu)
        pick_q = (lists[:, 2][:, None] == jnp.arange(QB, dtype=jnp.int32)[None, :]).astype(jnp.float32)
        summed = jnp.einsum("tq,taij->qaij", pick_q, term_parts, precision=lax.Precision.HIGHEST)
        return carry, summed.reshape(AUX_DEV, PANEL, PANEL).astype(jnp.bfloat16)

    unused, slab = lax.scan(fitted_input, jnp.float32(0.0), (ints_all, lists_all))
    fitted = jnp.dot(metric, slab.reshape(AUX, PANEL * PANEL), preferred_element_type=jnp.float32)
    fitted = fitted.astype(jnp.bfloat16).reshape(N_AUX, QB, AUXB, PANEL, PANEL)

    def accumulate(result, inputs):
        ints_dev, lists, fitted_dev = inputs
        mu_list = lists[:, 0]
        transformed = half_blocks(ints_dev, lists[:, 1], panel_dense).astype(jnp.float32)
        fitted_rows = fitted_dev[lists[:, 2]].astype(jnp.float32)
        row_terms = jnp.einsum("taim,taij->tmj", transformed, fitted_rows)
        pick_mu = (mu_list[:, None] == jnp.arange(MB, dtype=jnp.int32)[None, :]).astype(jnp.float32)
        result = result + jnp.einsum("tb,tmj->bmj", pick_mu, row_terms, precision=lax.Precision.HIGHEST)
        return result, jnp.float32(0.0)

    start = jnp.zeros((MB, SHELL, PANEL), jnp.float32)
    result, unused_two = lax.scan(accumulate, start, (ints_all, lists_all, fitted))
    return result[block_order]
```

```python
import jax
import jax.numpy as jnp
from jax import lax
from jax.experimental import pallas as pl
from jax.experimental.pallas import tpu as pltpu
from jax.sharding import PartitionSpec as P

MESH = pl.DeviceIdType.MESH
F32 = jnp.float32
BF16 = jnp.bfloat16
NY, NX, NC, NZ = 4, 4, 2, 8
NT, AB, SH, ORB, NSUP, NQ = 32, 8, 128, 16, 24, 16
JL = ORB // NC
HALF = NSUP // NC
LOADS = 8
PER_LOAD = NT // LOADS


def tables(screened_blocks, support, block_order):
    mu, nu, q = screened_blocks[:, 0], screened_blocks[:, 1], screened_blocks[:, 2]
    t = jnp.arange(NT, dtype=jnp.int32)
    before = t[None, :] < t[:, None]
    same_q = q[None, :] == q[:, None]
    rank = jnp.sum(((q[None, :] < q[:, None]) | (same_q & before)).astype(jnp.int32), axis=1)
    follows = jnp.max((same_q & before).astype(jnp.int32), axis=1)
    placed = (rank[None, :] == t[:, None]).astype(jnp.int32)
    order = jnp.sum(placed * t[None, :], axis=1)
    keep = jnp.sum(placed * follows[None, :], axis=1)
    nu_sorted = jnp.sum(placed * nu[None, :], axis=1)
    qs = jnp.arange(NQ, dtype=jnp.int32)
    last = jnp.maximum(jnp.sum((q[None, :] <= qs[:, None]).astype(jnp.int32), axis=1) - 1, 0)
    filled = jnp.max((q[None, :] == qs[:, None]).astype(jnp.int32), axis=1)
    second = jnp.max(((mu[None, :] == mu[:, None]) & before).astype(jnp.int32), axis=1)
    here = (block_order[:, None] == mu[None, :]).astype(jnp.int32)
    one, two = here * (1 - second)[None, :], here * second[None, :]
    t0, t1 = jnp.sum(one * t[None, :], axis=1), jnp.sum(two * t[None, :], axis=1)
    v0, v1 = jnp.sum(one, axis=1), jnp.sum(two, axis=1)
    blocks = jnp.arange(32, dtype=jnp.int32)
    entry = jnp.arange(NSUP, dtype=jnp.int32)
    hit = (support[:, None, :] == blocks[None, :, None]).astype(jnp.int32)
    pos = NSUP + jnp.sum(hit * (entry - NSUP)[None, None, :], axis=2)
    parts = [order, keep, nu_sorted, mu, nu, last, filled, q, q, t0, t1, v0, v1, pos.reshape(-1)]
    parts.append(jnp.zeros((1024 - 4 * 128 + 128 - 256,), jnp.int32))
    return jnp.concatenate(parts).reshape(8, 128)


def kernel(
    ints, coeff, metric, tab, out,
    iv, call, cown, c32, bst, bp, bsend, bps, rbuf, am, at, mg0, mg1, fs0, fs1, fr0, fr1,
    fxs, fxr, ft, bfull, gt, gs, gr, gx, gin, zall, tabr, stab,
    int_sem, own_sem, tab_sem, cs_s, cs_r, cf_s, cf_r, ms_s, ms_r, mf_s, mf_r,
    ex_s, ex_r, mg_s, mg_r, fr_s, fr_r, gx_s, gx_r, z_s, z_r,
):
    d = lax.axis_index("aux")
    z = lax.axis_index("occ")
    y, x, c = d // (NX * NC), (d // NC) % NX, d % NC

    def dev(yy, xx, cc, zz):
        return (yy * (NX * NC) + xx * NC + cc, zz)

    sibling = dev(y, x, 1 - c, z)

    def zpeer(k):
        return dev(y, x, c, (z + k) % NZ)

    def xpeer(k):
        return dev(y, (x + k) % NX, c, z)

    def ypeer(k):
        return dev((y + k) % NY, x, c, z)

    def plane(k):
        return (y + k // NX) % NY, (x + k % NX) % NX

    def copy(src, dst, s, r, to):
        return pltpu.make_async_remote_copy(
            src_ref=src, dst_ref=dst, send_sem=s, recv_sem=r, device_id=to, device_id_type=MESH
        )

    def load(i):
        part = pl.ds(i * PER_LOAD, PER_LOAD)
        return pltpu.make_async_copy(ints.at[part], iv.at[part], int_sem.at[i])

    for i in range(LOADS):
        load(i).start()
    own_tab = pltpu.make_async_copy(tab, stab.at[0], tab_sem.at[0])
    own_tab.start()
    for k in range(NY):
        cols = pl.ds(pl.multiple_of((k * NX + x) * 256, 256), 256)
        pltpu.make_async_copy(metric.at[:, cols], am.at[c, x, k], own_sem.at[0]).start()
        cols = pl.ds(pl.multiple_of((y * NX + k) * 256, 256), 256)
        pltpu.make_async_copy(metric.at[:, cols], at.at[c, y, k], own_sem.at[1]).start()

    barrier = pltpu.get_barrier_semaphore()
    partners = [sibling]
    partners += [zpeer(k) for k in range(1, NZ)]
    partners += [dev(*plane(k), c, z) for k in range(1, NX * NY)]
    for who in partners:
        pl.semaphore_signal(barrier, inc=1, device_id=who, device_id_type=MESH)

    for i in range(ORB):
        c32[pl.ds(i, NSUP, stride=ORB), :] = coeff[i].astype(F32)
    cown[:NSUP] = c32[...].astype(BF16).reshape(NSUP, ORB, SH)
    cown[NSUP] = jnp.zeros((ORB, SH), BF16)
    call[z] = cown[...]
    for k in range(NZ):
        call[k, NSUP] = jnp.zeros((ORB, SH), BF16)

    pl.semaphore_wait(barrier, len(partners))

    half = pl.ds(c * HALF, HALF)
    coeff_sends = []
    for k in (4, 3, 5, 2, 6, 1, 7):
        cp = copy(cown.at[half], call.at[z, half], cs_s.at[k - 1], cs_r.at[k - 1], zpeer(k))
        cp.start()
        coeff_sends.append(cp)
    tab_send = copy(tab, tabr, ex_s.at[0], ex_r.at[0], sibling)
    tab_send.start()
    for k in (2, 1, 3):
        for m in range(NY):
            cols = pl.ds(pl.multiple_of((m * NX + (x + k) % NX) * 256, 256), 256)
            copy(metric.at[:, cols], am.at[c, x, m], ms_s.at[0, k - 1], ms_r.at[0, k - 1], xpeer(k)).start()
            cols = pl.ds(pl.multiple_of(((y + k) % NY * NX + m) * 256, 256), 256)
            copy(metric.at[:, cols], at.at[c, y, m], ms_s.at[1, k - 1], ms_r.at[1, k - 1], ypeer(k)).start()

    own_tab.wait()

    def entry(o, b):
        return stab[0, 3 + o // 4, (o % 4) * 32 + b]

    def half_transform(t, st):
        own = cown[entry(z, stab[0, 0, 96 + t])]
        rhs = jnp.concatenate([iv[t, a] for a in range(AB)], axis=1)
        res = jnp.dot(own, rhs, preferred_element_type=F32)
        for a in range(AB):
            bst[st, pl.ds(a, ORB, stride=AB), :] = res[:, a * SH : (a + 1) * SH]
        bp[t] = bst[st].astype(BF16)

    @pl.loop(0, LOADS)
    def _(i):
        load(i).wait()
        for u in range(PER_LOAD):
            half_transform(i * PER_LOAD + u, u)

    rows_c = pl.ds(pl.multiple_of(c * 64, 64), 64)
    rows_n = pl.ds(pl.multiple_of((1 - c) * 64, 64), 64)

    @pl.loop(0, NT, unroll=4)
    def _(k):
        bsend[k] = bp[stab[0, 0, k], rows_n, :]

    b_send = copy(bsend, bps.at[1], ex_s.at[1], ex_r.at[1], sibling)
    b_send.start()

    @pl.loop(0, NT, unroll=4)
    def _(k):
        bps[0, k] = bp[stab[0, 0, k], rows_c, :]

    forwards = []
    for k in (1, 7, 2, 6, 3, 5, 4):
        src = (z + NZ - k) % NZ
        got = call.at[src, half]
        copy(got, got, cs_s.at[k - 1], cs_r.at[k - 1], zpeer(k)).wait_recv()
        cp = copy(got, got, cf_s.at[k - 1], cf_r.at[k - 1], sibling)
        cp.start()
        forwards.append(cp)
    tab_send.wait_recv()
    sib_tab = pltpu.make_async_copy(tabr, stab.at[1], tab_sem.at[1])
    sib_tab.start()
    sib_tab.wait()
    other = pl.ds((1 - c) * HALF, HALF)
    for k in (1, 7, 2, 6, 3, 5, 4):
        src = (z + NZ - k) % NZ
        got = call.at[src, other]
        copy(got, got, cf_s.at[k - 1], cf_r.at[k - 1], sibling).wait_recv()
    b_send.wait_recv()

    def pick(flag, value):
        return jnp.where(jnp.full(value.shape, flag, jnp.int32) == 1, value, 0.0)

    def panel(b):
        return jnp.concatenate([call[o, entry(o, b)] for o in range(NZ)], axis=0)

    nt = (((1,), (1,)), ((), ()))

    for s in range(NC):
        rbuf[s, 0] = jnp.zeros((64, SH), F32)

    @pl.loop(0, NT, unroll=2)
    def _(k):
        for s in range(NC):
            term = lax.dot_general(bps[s, k], panel(stab[s, 0, 64 + k]), nt, preferred_element_type=F32)
            rbuf[s, k + 1] = term + pick(stab[s, 0, 32 + k], rbuf[s, k])

    for s in range(NC):
        base = (c if s == 0 else 1 - c) * 128

        @pl.loop(0, NQ // 2, unroll=2)
        def _(h):
            got = []
            for u in range(2):
                blk = rbuf[s, stab[s, 1, 32 + 2 * h + u] + 1]
                got.append(pick(stab[s, 1, 48 + 2 * h + u], blk).reshape(JL, AB, SH))
            both = jnp.concatenate(got, axis=1).astype(BF16)
            rows = pl.ds(pl.multiple_of(base + h * 16, 16), 16)
            mg0[y, :, rows, :] = both[:4]
            mg1[x, :, rows, :] = both[4:]

    def m_copy(h, k, j):
        me, buf, to = ((y, mg0, ypeer(k)), (x, mg1, xpeer(k)))[h]
        part = buf.at[me, pl.ds(2 * j, 2)]
        return copy(part, part, mg_s.at[h, k - 1, j], mg_r.at[h, k - 1, j], to)

    def m_wait(h, k, j):
        me, buf, to = ((y, mg0, ypeer(k)), (x, mg1, xpeer(k)))[h]
        part = buf.at[(me + 4 - k) % 4, pl.ds(2 * j, 2)]
        copy(part, part, mg_s.at[h, k - 1, j], mg_r.at[h, k - 1, j], to).wait_recv()

    for j in range(2):
        for k in (2, 1, 3):
            for h in range(2):
                m_copy(h, k, j).start()

    pltpu.make_async_copy(am.at[c, x], am.at[c, x], own_sem.at[0]).wait()
    pltpu.make_async_copy(at.at[c, y], at.at[c, y], own_sem.at[1]).wait()
    for k in range(4):
        for h, (buf, me) in enumerate(((am, x), (at, y))):
            part = buf.at[c, (me + 4 - k) % 4]
            if k > 0:
                copy(part, part, ms_s.at[h, k - 1], ms_r.at[h, k - 1], sibling).wait_recv()
            copy(part, part, mf_s.at[h, k], mf_r.at[h, k], sibling).start()

    @pl.loop(0, NT)
    def _(t):
        rows = panel(stab[0, 1, t])
        for a in range(AB):
            blk = lax.dot_general(rows, iv[t, a], nt, preferred_element_type=F32)
            bfull[t, pl.ds(a * SH, SH), :] = blk.astype(BF16)

    for k in range(4):
        for h, (buf, me) in enumerate(((am, x), (at, y))):
            part = buf.at[1 - c, (me + 4 - k) % 4]
            copy(part, part, mf_s.at[h, k], mf_r.at[h, k], sibling).wait_recv()

    def f_copy(h, k, j):
        src, dst, to = ((fs0, fr0, xpeer(k)), (fs1, fr1, ypeer(k)))[h]
        part = pl.ds(2 * j, 2)
        return copy(src.at[k, part], dst.at[k, part], fr_s.at[h, k - 1, j], fr_r.at[h, k - 1, j], to)

    def fit(h, k, j):
        mat, got, dst, me = ((am, mg0, fs0, x), (at, mg1, fs1, y))[h]
        row = (me + k) % 4
        total = None
        for m in range(4):
            lhs = jnp.concatenate([mat[0, row, m], mat[1, row, m]], axis=0)
            rhs = jnp.concatenate([got[m, 2 * j], got[m, 2 * j + 1]], axis=1)
            term = jnp.dot(lhs, rhs, preferred_element_type=F32)
            total = term if total is None else total + term
        total = total.astype(BF16)
        dst[k, 2 * j] = total[:, :SH]
        dst[k, 2 * j + 1] = total[:, SH:]

    for j in range(2):
        for h in range(2):
            for k in (1, 3, 2):
                m_wait(h, k, j)
        for k in (2, 1, 3):
            for h in range(2):
                fit(h, k, j)
                f_copy(h, k, j).start()
        for h in range(2):
            fit(h, 0, j)

    own_rows = pl.ds(pl.multiple_of(c * 128, 128), 128)
    sib_rows = pl.ds(pl.multiple_of((1 - c) * 128, 128), 128)

    def total_of(h, jj, rows):
        src, got = ((fs0, fr0), (fs1, fr1))[h]
        total = src[0, jj, rows, :].astype(F32)
        for k in range(1, 4):
            total = total + got[k, jj, rows, :].astype(F32)
        return total

    fx = copy(fxs, fxr, ex_s.at[2], ex_r.at[2], sibling)
    for j in range(2):
        for h in range(2):
            for k in (1, 3, 2):
                f_copy(h, k, j).wait_recv()
            for u in range(2):
                fxs[4 * h + 2 * j + u] = total_of(h, 2 * j + u, sib_rows).astype(BF16)
    fx.start()
    for h in range(2):
        for jj in range(4):
            ft[pl.ds(4 * h + jj, 128, stride=ORB), :] = total_of(h, jj, own_rows)
    fx.wait_recv()
    for jj in range(JL):
        ft[pl.ds(JL + jj, 128, stride=ORB), :] = fxr[jj].astype(F32)

    ftq = ft.reshape(NQ, AB * ORB, SH)
    low = pl.ds(pl.multiple_of(c * JL, JL), JL)
    high = pl.ds(pl.multiple_of((1 - c) * JL, JL), JL)

    @pl.loop(0, NT, unroll=2)
    def _(t):
        rows = ftq[stab[0, 1, 64 + t]]
        lhs = jnp.concatenate([rows[a * ORB : (a + 1) * ORB] for a in range(AB)], axis=1)
        lhs = lhs.astype(BF16)
        res = jnp.dot(lhs, bfull[t], preferred_element_type=F32)
        gt[t, low, :] = res[:JL]
        gt[t, high, :] = res[JL:]

    for s in range(32):
        a = pick(stab[0, 2, 64 + s], gt[stab[0, 2, s]])
        b = pick(stab[0, 2, 96 + s], gt[stab[0, 2, 32 + s]])
        gs[s % 2, s // 2] = a + b

    g_send = copy(gs.at[1 - c], gr, ex_s.at[3], ex_r.at[3], sibling)
    g_send.start()
    g_send.wait_recv()
    gx[...] = gs[c] + gr[...]
    sends = []
    for k in (10, 6, 14, 9, 11, 5, 7, 13, 15, 2, 8, 1, 3, 4, 12):
        yy, xx = plane(k)
        cp = copy(gx.at[yy * NX + xx], gin.at[k], gx_s.at[k - 1], gx_r.at[k - 1], dev(yy, xx, c, z))
        cp.start()
        sends.append(cp)
    total = gx[y * NX + x]
    for k in (1, 3, 4, 12, 2, 8, 5, 7, 13, 15, 6, 14, 9, 11, 10):
        copy(gx.at[0], gin.at[k], gx_s.at[k - 1], gx_r.at[k - 1], sibling).wait_recv()
        total = total + gin[k]
    zall[z] = total
    for k in (4, 3, 5, 2, 6, 1, 7):
        cp = copy(zall.at[z], zall.at[z], z_s.at[k - 1], z_r.at[k - 1], zpeer(k))
        cp.start()
        sends.append(cp)
    for k in (1, 7, 2, 6, 3, 5, 4):
        got = zall.at[(z + NZ - k) % NZ]
        copy(got, got, z_s.at[k - 1], z_r.at[k - 1], zpeer(k)).wait_recv()
    out[...] = zall[...].reshape(NZ * ORB, SH).T

    for cp in coeff_sends + forwards + [tab_send, b_send, fx, g_send] + sends:
        cp.wait_send()
    for k in range(4):
        for h, (buf, me) in enumerate(((am, x), (at, y))):
            part = buf.at[c, (me + 4 - k) % 4]
            if k > 0:
                copy(part, part, ms_s.at[h, k - 1], ms_r.at[h, k - 1], sibling).wait_send()
            copy(part, part, mf_s.at[h, k], mf_r.at[h, k], sibling).wait_send()
    for j in range(2):
        for k in (2, 1, 3):
            for h in range(2):
                m_copy(h, k, j).wait_send()
                f_copy(h, k, j).wait_send()


def body(integrals, screened_blocks, coeff, support, metric, block_order):
    tab = tables(screened_blocks, support, block_order)
    vm = pltpu.VMEM
    dma = pltpu.SemaphoreType.DMA
    any_spec = pl.BlockSpec(memory_space=pl.ANY)
    vmem_spec = pl.BlockSpec(memory_space=pltpu.VMEM)
    res = pl.pallas_call(
        kernel,
        out_shape=jax.ShapeDtypeStruct((SH, NZ * ORB), F32),
        in_specs=[any_spec, vmem_spec, any_spec, vmem_spec],
        out_specs=vmem_spec,
        scratch_shapes=[
            vm((NT, AB, SH, SH), BF16),
            vm((NZ, NSUP + 1, ORB, SH), BF16),
            vm((NSUP + 1, ORB, SH), BF16),
            vm((NSUP * ORB, SH), F32),
            vm((PER_LOAD, 128, SH), F32),
            vm((NT, 128, SH), BF16),
            vm((NT, 64, SH), BF16),
            vm((NC, NT, 64, SH), BF16),
            vm((NC, NT + 1, 64, SH), F32),
            vm((NC, 4, 4, 128, 256), BF16),
            vm((NC, 4, 4, 128, 256), BF16),
            vm((4, 4, 256, SH), BF16),
            vm((4, 4, 256, SH), BF16),
            vm((4, 4, 256, SH), BF16),
            vm((4, 4, 256, SH), BF16),
            vm((4, 4, 256, SH), BF16),
            vm((4, 4, 256, SH), BF16),
            vm((JL, 128, SH), BF16),
            vm((JL, 128, SH), BF16),
            vm((128 * ORB, SH), F32),
            vm((NT, AB * SH, SH), BF16),
            vm((NT, ORB, SH), F32),
            vm((NC, 16, ORB, SH), F32),
            vm((16, ORB, SH), F32),
            vm((16, ORB, SH), F32),
            vm((16, ORB, SH), F32),
            vm((NZ, ORB, SH), F32),
            vm((8, 128), jnp.int32),
            pltpu.SMEM((2, 8, 128), jnp.int32),
            dma((LOADS,)), dma((2,)), dma((2,)),
            dma((7,)), dma((7,)), dma((7,)), dma((7,)),
            dma((2, 3)), dma((2, 3)), dma((2, 4)), dma((2, 4)),
            dma((4,)), dma((4,)),
            dma((2, 3, 2)), dma((2, 3, 2)), dma((2, 3, 2)), dma((2, 3, 2)),
            dma((15,)), dma((15,)), dma((7,)), dma((7,)),
        ],
        compiler_params=pltpu.CompilerParams(
            collective_id=0, has_side_effects=True, vmem_limit_bytes=56 * 1024 * 1024
        ),
        cost_estimate=pl.CostEstimate(flops=4 * 10**9, bytes_accessed=10 * 10**6, transcendentals=0),
        name="exchange",
    )(integrals, coeff, metric, tab)
    return res[None]


def solution(mesh):
    in_specs = (
        P("aux", None, None, None),
        P("aux", None),
        P("occ", None, None),
        P(),
        P("aux", None),
        P(),
    )
    return jax.shard_map(
        body, mesh=mesh, in_specs=in_specs, out_specs=P("aux", None, None), check_vma=False
    )
```

```python
import jax
import jax.numpy as jnp
from jax import lax
from jax.experimental import pallas as pl
from jax.experimental.pallas import tpu as pltpu
from jax.sharding import PartitionSpec as P

MESH = pl.DeviceIdType.MESH
F32 = jnp.float32
BF16 = jnp.bfloat16
I32 = jnp.int32
NY, NX, NC, NZ = 4, 4, 2, 8
NT, AB, SH, ORB, NSUP, NQ = 32, 8, 128, 16, 24, 16
JL = ORB // NC
PIECE = NSUP // (NX * NC)
LOADS = 8
PER_LOAD = NT // LOADS
ORDER, KEEP, NUS, MU, NU, LAST, FILLED, QQ, T0, T1, V0, V1, POS = 0, 1, 2, 3, 4, 5, 6, 7, 8, 9, 10, 11, 16
BATCHES = ((1, 2), (6, 2), (3, 3))


def fill_tables(sbv, suv, bov, tabv):
    t = lax.broadcasted_iota(I32, (NT, NT), 0)
    lane = lax.broadcasted_iota(I32, (NT, NT), 1)
    mu, nu, q = [jnp.broadcast_to(sbv[:, i : i + 1], (NT, NT)) for i in range(3)]

    def down(mask, value):
        return jnp.sum(jnp.where(mask, value, 0), axis=0, keepdims=True)

    def across(mask):
        return jnp.sum(jnp.where(mask, 1, 0), axis=1, keepdims=True)

    diagonal, before = t == lane, lane < t
    mu_r, nu_r, q_r = [down(diagonal, v) for v in (mu, nu, q)]
    rank = across((q_r < q) | ((q_r == q) & before))
    follows = across((q_r == q) & before)
    second = across((mu_r == mu) & before)
    placed = rank == lane
    here = bov[...] == mu
    one, two = here & (second == 0), here & (second > 0)
    rows = {
        ORDER: down(placed, t),
        KEEP: down(placed & (follows > 0), 1),
        NUS: down(placed, nu),
        MU: mu_r,
        NU: nu_r,
        LAST: jnp.maximum(down(q <= lane, 1) - 1, 0),
        FILLED: jnp.minimum(down(q == lane, 1), 1),
        QQ: q_r,
        T0: jnp.max(jnp.where(one, t, 0), axis=0, keepdims=True),
        T1: jnp.max(jnp.where(two, t, 0), axis=0, keepdims=True),
        V0: down(one, 1),
        V1: down(two, 1),
    }
    for i, v in rows.items():
        tabv[i : i + 1, 0:NT] = v
    block = lax.broadcasted_iota(I32, (NZ, 32), 1)
    pos = jnp.full((NZ, 32), NSUP, I32)
    for s in range(NSUP):
        pos = jnp.where(jnp.broadcast_to(suv[:, s : s + 1], (NZ, 32)) == block, s, pos)
    tabv[POS : POS + NZ, 0:32] = pos


def kernel(
    ints, coeff, metric, sb, support, border, out,
    cin, sbv, suv, bov, tabv, tabr, stab,
    iv, call, cown, c32, bst, bp, bsend, bps, rbuf, am, at, mg0, mg1, fo, fsend, frelay, fplain, fsum,
    fxs, fxr, ft, bfull, gt, gs, gr, gx, gin, zall,
    in_sem, int_sem, tab_sem, zc_s, zc_r, xc_s, xc_r, cc_s, cc_r, ms_s, ms_r, mf_s, mf_r,
    ex_s, ex_r, mg_s, mg_r, mw_s, mw_r, fp_s, fp_r, gx_s, gx_r, z_s, z_r,
):
    d = lax.axis_index("aux")
    z = lax.axis_index("occ")
    y, x, c = d // (NX * NC), (d // NC) % NX, d % NC

    def dev(yy, xx, cc, zz):
        return (yy * (NX * NC) + xx * NC + cc, zz)

    sibling = dev(y, x, 1 - c, z)

    def zpeer(k):
        return dev(y, x, c, (z + k) % NZ)

    def xpeer(k):
        return dev(y, (x + k) % NX, c, z)

    def ypeer(k):
        return dev((y + k) % NY, x, c, z)

    def plane(k):
        return (y + k // NX) % NY, (x + k % NX) % NX

    def copy(src, dst, s, r, to):
        return pltpu.make_async_remote_copy(
            src_ref=src, dst_ref=dst, send_sem=s, recv_sem=r, device_id=to, device_id_type=MESH
        )

    pending = []

    def start(cp):
        cp.start()
        pending.append(cp)
        return cp

    def load(i):
        part = pl.ds(i * PER_LOAD, PER_LOAD)
        return pltpu.make_async_copy(ints.at[part], iv.at[part], int_sem.at[i])

    small = [
        pltpu.make_async_copy(src, dst, in_sem.at[i])
        for i, (src, dst) in enumerate(((coeff, cin), (sb, sbv), (support, suv), (border, bov)))
    ]
    for cp in small:
        cp.start()
    barrier = pltpu.get_barrier_semaphore()
    partners = [zpeer(k) for k in (4, 3, 5, 2, 6, 1, 7)]
    partners += [dev(*plane(k), c, z) for k in range(1, NX * NY)]
    partners += [sibling]
    for who in partners:
        pl.semaphore_signal(barrier, inc=1, device_id=who, device_id_type=MESH)
    for i in range(LOADS):
        load(i).start()

    def metric_cols(k, m):
        return metric.at[:, pl.ds(pl.multiple_of(((y + k) % NY * NX + m) * 256, 256), 256)]

    for m in range(NX):
        pltpu.make_async_copy(metric_cols(0, m), at.at[c, y, m], in_sem.at[4]).start()

    small[0].wait()
    for i in range(ORB):
        c32[pl.ds(i, NSUP, stride=ORB), :] = cin[i].astype(F32)
    cown[:NSUP] = c32[...].astype(BF16).reshape(NSUP, ORB, SH)
    cown[NSUP] = jnp.zeros((ORB, SH), BF16)
    call[0] = cown[...]
    for k in range(1, NZ):
        call[k, NSUP] = jnp.zeros((ORB, SH), BF16)
    tabv[...] = jnp.zeros(tabv.shape, I32)
    for cp in small[1:]:
        cp.wait()

    pl.semaphore_wait(barrier, len(partners))

    def piece(k):
        return pl.ds(PIECE * (NC * ((x + NX - k) % NX) + c), PIECE)

    for k in (4, 3, 5, 2, 6, 1, 7):
        start(copy(cown.at[piece(0)], call.at[NZ - k, piece(0)], zc_s.at[k - 1], zc_r.at[k - 1], zpeer(k)))
    for k in (2, 1, 3):
        for m in range(NX):
            copy(metric_cols(k, m), at.at[c, y, m], ms_s.at[k - 1], ms_r.at[k - 1], ypeer(k)).start()
        pending.append(copy(at.at[c, y], at.at[c, y], ms_s.at[k - 1], ms_r.at[k - 1], ypeer(k)))

    fill_tables(sbv, suv, bov, tabv)
    own_tab = pltpu.make_async_copy(tabv, stab.at[0], tab_sem.at[0])
    own_tab.start()
    tab_send = start(copy(tabv, tabr, ex_s.at[0], ex_r.at[0], sibling))
    own_tab.wait()

    zr = [(z + r) % NZ for r in range(NZ)]

    def entry(r, b):
        return stab[0, POS + zr[r], b]

    def half_transform(t, st):
        own = cown[entry(0, stab[0, MU, t])]
        rhs = jnp.concatenate([iv[t, a] for a in range(AB)], axis=1)
        res = jnp.dot(own, rhs, preferred_element_type=F32)
        for a in range(AB):
            bst[st, pl.ds(a, ORB, stride=AB), :] = res[:, a * SH : (a + 1) * SH]
        bp[t] = bst[st].astype(BF16)

    def half_loads(lo, hi):
        @pl.loop(lo, hi)
        def _(i):
            load(i).wait()
            for u in range(PER_LOAD):
                half_transform(i * PER_LOAD + u, u)

    def zwait(r):
        got = call.at[r, piece(0)]
        copy(got, got, zc_s.at[NZ - r - 1], zc_r.at[NZ - r - 1], sibling).wait_recv()

    def spread(b):
        lo, n = BATCHES[b]
        part = call.at[pl.ds(lo, n), piece(0)]
        for k in (2, 1, 3):
            start(copy(part, part, xc_s.at[k - 1, b], xc_r.at[k - 1, b], xpeer(k)))
        start(copy(part, part, cc_s.at[0, b], cc_r.at[0, b], sibling))

    def relay(k, b):
        lo, n = BATCHES[b]
        part = call.at[pl.ds(lo, n), piece(k)]
        copy(part, part, xc_s.at[k - 1, b], xc_r.at[k - 1, b], sibling).wait_recv()
        start(copy(part, part, cc_s.at[k, b], cc_r.at[k, b], sibling))

    half_loads(0, LOADS // 2)
    zwait(1)
    zwait(2)
    spread(0)
    zwait(7)
    zwait(6)
    spread(1)
    half_loads(LOADS // 2, LOADS)
    for r in (3, 5, 4):
        zwait(r)
    spread(2)

    rows_c = pl.ds(pl.multiple_of(c * 64, 64), 64)
    rows_n = pl.ds(pl.multiple_of((1 - c) * 64, 64), 64)

    @pl.loop(0, NT, unroll=4)
    def _(k):
        bsend[k] = bp[stab[0, ORDER, k], rows_n, :]

    b_send = start(copy(bsend, bps.at[1], ex_s.at[1], ex_r.at[1], sibling))

    @pl.loop(0, NT, unroll=4)
    def _(k):
        bps[0, k] = bp[stab[0, ORDER, k], rows_c, :]

    tab_send.wait_recv()
    sib_tab = pltpu.make_async_copy(tabr, stab.at[1], tab_sem.at[1])
    sib_tab.start()
    sib_tab.wait()
    for b in range(3):
        for k in (1, 3, 2):
            relay(k, b)
    for b in range(3):
        for k in (0, 1, 3, 2):
            lo, n = BATCHES[b]
            part = call.at[pl.ds(lo, n), pl.ds(PIECE * (NC * ((x + NX - k) % NX) + 1 - c), PIECE)]
            copy(part, part, cc_s.at[k, b], cc_r.at[k, b], sibling).wait_recv()

    def pick(flag, value):
        return jnp.where(jnp.full(value.shape, flag, I32) == 1, value, 0.0)

    def panel(b):
        return jnp.concatenate([call[r, entry(r, b)] for r in range(NZ)], axis=0)

    nt = (((1,), (1,)), ((), ()))

    def m_rows(s):
        base = (c if s == 0 else 1 - c) * 128
        return pl.ds(pl.multiple_of(base, 128), 128)

    def m_part(h, me, j, s):
        return (mg0, mg1)[h].at[me, pl.ds(2 * j, 2), m_rows(s)]

    def ring(h):
        return (y, ypeer) if h == 0 else (x, xpeer)

    def m_copy(h, w, j, s):
        me, to = ring(h)
        part = m_part(h, me, j, s)
        return copy(part, part, mg_s.at[h, w, j, s], mg_r.at[h, w, j, s], to(1 if w == 0 else 3))

    def m_wait(h, w, j, s):
        me, to = ring(h)
        part = m_part(h, (me + (3 if w == 0 else 1)) % 4, j, s)
        copy(part, part, mg_s.at[h, w, j, s], mg_r.at[h, w, j, s], sibling).wait_recv()

    def m_forward(h, j, s):
        me, to = ring(h)
        m_wait(h, j, j, s)
        part = m_part(h, (me + (3 if j == 0 else 1)) % 4, j, s)
        start(copy(part, part, mw_s.at[h, j, s], mw_r.at[h, j, s], to(1 if j == 0 else 3)))

    def m_far(h, j, s):
        me, to = ring(h)
        part = m_part(h, (me + 2) % 4, j, s)
        copy(part, part, mw_s.at[h, j, s], mw_r.at[h, j, s], sibling).wait_recv()

    for s in range(NC):
        if s == 1:
            b_send.wait_recv()
        rbuf[s, 0] = jnp.zeros((64, SH), F32)

        @pl.loop(0, NT, unroll=4)
        def _(k):
            term = lax.dot_general(bps[s, k], panel(stab[s, NUS, k]), nt, preferred_element_type=F32)
            rbuf[s, k + 1] = term + pick(stab[s, KEEP, k], rbuf[s, k])

        for h in range(NQ // 2):
            got = []
            for u in range(2):
                blk = rbuf[s, stab[s, LAST, 2 * h + u] + 1]
                got.append(pick(stab[s, FILLED, 2 * h + u], blk).reshape(JL, AB, SH))
            both = jnp.concatenate(got, axis=1).astype(BF16)
            rows = pl.ds(pl.multiple_of((c if s == 0 else 1 - c) * 128 + h * 16, 16), 16)
            mg0[y, :, rows, :] = both[:4]
            mg1[x, :, rows, :] = both[4:]
        for i in range(2):
            for h in range(2):
                start(m_copy(h, 0, i, s))
                start(m_copy(h, 1, 1 - i, s))

    pltpu.make_async_copy(at.at[c, y], at.at[c, y], in_sem.at[4]).wait()
    for k in range(4):
        part = at.at[c, (y + 4 - k) % 4]
        if k > 0:
            copy(part, part, ms_s.at[k - 1], ms_r.at[k - 1], sibling).wait_recv()
        start(copy(part, part, mf_s.at[k], mf_r.at[k], sibling))

    def full_blocks(lo, hi):
        @pl.loop(lo, hi)
        def _(t):
            rhs = iv[t].reshape(AB * SH, SH)
            blk = lax.dot_general(panel(stab[0, NU, t]), rhs, nt, preferred_element_type=F32).astype(BF16)
            for a in range(AB):
                bfull[t, pl.ds(a * SH, SH), :] = blk[:, a * SH : (a + 1) * SH]

    full_blocks(0, 6)
    for j in range(2):
        for h in range(2):
            m_forward(h, j, 0)
    full_blocks(6, 14)
    for j in range(2):
        for h in range(2):
            m_forward(h, j, 1)
    full_blocks(14, NT)
    for k in range(4):
        part = at.at[1 - c, (y + 4 - k) % 4]
        copy(part, part, mf_s.at[k], mf_r.at[k], sibling).wait_recv()

    @pl.loop(0, NY)
    def _(yy):
        for cc in range(NC):
            for xx in range(NX):
                am[yy, cc, pl.ds(xx * 256, 256), :] = at[cc, yy, xx].T

    def fit(h, j):
        got = (mg0, mg1)[h]
        rhs = [jnp.concatenate([got[m, 2 * j], got[m, 2 * j + 1]], axis=1) for m in range(4)]
        rhs = jnp.concatenate(rhs, axis=0)
        if h == 0:
            lhs = jnp.concatenate([am[m, cc] for m in range(4) for cc in range(NC)], axis=1)
        else:
            lhs = jnp.concatenate(
                [
                    jnp.concatenate([at[cc, yy, m] for m in range(4)], axis=1)
                    for yy in range(NY)
                    for cc in range(NC)
                ],
                axis=0,
            )
        res = jnp.dot(lhs, rhs, preferred_element_type=F32)
        for r in range(4):
            fo[h, j, r, 0] = res[r * 256 : (r + 1) * 256, :SH]
            fo[h, j, r, 1] = res[r * 256 : (r + 1) * 256, SH:]

    def f_copy(h, j, kind):
        me, to = ring(1 - h)
        right = (j == 0) == (kind != 1)
        dst = (frelay, fplain, fsum)[kind]
        return copy(
            fsend.at[h, j, kind], dst.at[h, j], fp_s.at[h, j, kind], fp_r.at[h, j, kind], to(1 if right else 3)
        )

    def f_send(h, j, kind):
        me, to = ring(1 - h)
        off = (2, 3 if j == 0 else 1, 1 if j == 0 else 3)[kind]
        part = fo[h, j, (me + off) % 4]
        if kind == 2:
            f_copy(h, j, 0).wait_recv()
            part = part + frelay[h, j].astype(F32)
        fsend[h, j, kind] = part.astype(BF16)
        start(f_copy(h, j, kind))

    for j in range(2):
        for h in range(2):
            for s in range(NC):
                m_wait(h, 1 - j, j, s)
                m_far(h, j, s)
            fit(h, j)
            f_send(h, j, 0)
            f_send(h, j, 1)
    for j in range(2):
        for h in range(2):
            f_send(h, j, 2)

    own_rows = pl.ds(pl.multiple_of(c * 128, 128), 128)
    sib_rows = pl.ds(pl.multiple_of((1 - c) * 128, 128), 128)

    def total_of(h, j, u, rows):
        me, to = ring(1 - h)
        total = fo[h, j, me, u, rows, :] + fplain[h, j, u, rows, :].astype(F32)
        return total + fsum[h, j, u, rows, :].astype(F32)

    def fx(j):
        part = pl.ds(4 * j, 4)
        return copy(fxs.at[part], fxr.at[part], ex_s.at[2 + j], ex_r.at[2 + j], sibling)

    for j in range(2):
        for h in range(2):
            f_copy(h, j, 1).wait_recv()
            f_copy(h, j, 2).wait_recv()
            for u in range(2):
                fxs[4 * j + 2 * h + u] = total_of(h, j, u, sib_rows).astype(BF16)
        start(fx(j))
        for h in range(2):
            for u in range(2):
                ft[pl.ds(4 * h + 2 * j + u, 128, stride=ORB), :] = total_of(h, j, u, own_rows)
    for j in range(2):
        fx(j).wait_recv()
        for h in range(2):
            for u in range(2):
                ft[pl.ds(JL + 4 * h + 2 * j + u, 128, stride=ORB), :] = fxr[4 * j + 2 * h + u].astype(F32)

    ftq = ft.reshape(NQ, AB * ORB, SH)
    low = pl.ds(pl.multiple_of(c * JL, JL), JL)
    high = pl.ds(pl.multiple_of((1 - c) * JL, JL), JL)

    @pl.loop(0, NT, unroll=8)
    def _(t):
        rows = ftq[stab[0, QQ, t]]
        lhs = jnp.concatenate([rows[a * ORB : (a + 1) * ORB] for a in range(AB)], axis=1)
        res = jnp.dot(lhs.astype(BF16), bfull[t], preferred_element_type=F32)
        gt[t, low, :] = res[:JL]
        gt[t, high, :] = res[JL:]

    for s in range(32):
        one = pick(stab[0, V0, s], gt[stab[0, T0, s]])
        two = pick(stab[0, V1, s], gt[stab[0, T1, s]])
        gs[s % 2, s // 2] = one + two

    g_send = start(copy(gs.at[1 - c], gr, ex_s.at[4], ex_r.at[4], sibling))
    g_send.wait_recv()
    gx[...] = gs[c] + gr[...]
    for k in (10, 6, 14, 9, 11, 5, 7, 13, 15, 2, 8, 1, 3, 4, 12):
        yy, xx = plane(k)
        start(copy(gx.at[yy * NX + xx], gin.at[k], gx_s.at[k - 1], gx_r.at[k - 1], dev(yy, xx, c, z)))
    total = gx[y * NX + x]
    for k in (1, 3, 4, 12, 2, 8, 5, 7, 13, 15, 6, 14, 9, 11, 10):
        copy(gx.at[0], gin.at[k], gx_s.at[k - 1], gx_r.at[k - 1], sibling).wait_recv()
        total = total + gin[k]
    zall[z] = total
    for k in (4, 3, 5, 2, 6, 1, 7):
        start(copy(zall.at[z], zall.at[z], z_s.at[k - 1], z_r.at[k - 1], zpeer(k)))
    for k in (1, 7, 2, 6, 3, 5, 4):
        got = zall.at[(z + NZ - k) % NZ]
        copy(got, got, z_s.at[k - 1], z_r.at[k - 1], zpeer(k)).wait_recv()
    out[...] = zall[...].reshape(NZ * ORB, SH).T

    for cp in pending:
        cp.wait_send()


def body(integrals, screened_blocks, coeff, support, metric, block_order):
    vm = pltpu.VMEM
    dma = pltpu.SemaphoreType.DMA
    any_spec = pl.BlockSpec(memory_space=pl.ANY)
    res = pl.pallas_call(
        kernel,
        out_shape=jax.ShapeDtypeStruct((SH, NZ * ORB), F32),
        in_specs=[any_spec] * 6,
        out_specs=pl.BlockSpec(memory_space=pltpu.VMEM),
        scratch_shapes=[
            vm((ORB, NSUP, SH), BF16),
            vm((NT, 3), I32),
            vm((NZ, NSUP), I32),
            vm((1, 32), I32),
            vm((24, 128), I32),
            vm((24, 128), I32),
            pltpu.SMEM((2, 24, 128), I32),
            vm((NT, AB, SH, SH), BF16),
            vm((NZ, NSUP + 1, ORB, SH), BF16),
            vm((NSUP + 1, ORB, SH), BF16),
            vm((NSUP * ORB, SH), F32),
            vm((PER_LOAD, 128, SH), F32),
            vm((NT, 128, SH), BF16),
            vm((NT, 64, SH), BF16),
            vm((NC, NT, 64, SH), BF16),
            vm((NC, NT + 1, 64, SH), F32),
            vm((NY, NC, 1024, SH), BF16),
            vm((NC, 4, 4, 128, 256), BF16),
            vm((4, 4, 256, SH), BF16),
            vm((4, 4, 256, SH), BF16),
            vm((2, 2, 4, 2, 256, SH), F32),
            vm((2, 2, 3, 2, 256, SH), BF16),
            vm((2, 2, 2, 256, SH), BF16),
            vm((2, 2, 2, 256, SH), BF16),
            vm((2, 2, 2, 256, SH), BF16),
            vm((JL, 128, SH), BF16),
            vm((JL, 128, SH), BF16),
            vm((128 * ORB, SH), F32),
            vm((NT, AB * SH, SH), BF16),
            vm((NT, ORB, SH), F32),
            vm((NC, 16, ORB, SH), F32),
            vm((16, ORB, SH), F32),
            vm((16, ORB, SH), F32),
            vm((16, ORB, SH), F32),
            vm((NZ, ORB, SH), F32),
            dma((5,)), dma((LOADS,)), dma((2,)),
            dma((7,)), dma((7,)), dma((3, 3)), dma((3, 3)), dma((4, 3)), dma((4, 3)),
            dma((3,)), dma((3,)), dma((4,)), dma((4,)),
            dma((5,)), dma((5,)),
            dma((2, 2, 2, 2)), dma((2, 2, 2, 2)), dma((2, 2, 2)), dma((2, 2, 2)),
            dma((2, 2, 3)), dma((2, 2, 3)),
            dma((15,)), dma((15,)), dma((7,)), dma((7,)),
        ],
        compiler_params=pltpu.CompilerParams(
            collective_id=0, has_side_effects=True, vmem_limit_bytes=56 * 1024 * 1024
        ),
        cost_estimate=pl.CostEstimate(flops=4 * 10**9, bytes_accessed=10 * 10**6, transcendentals=0),
        name="exchange",
    )(integrals, coeff, metric, screened_blocks, support, block_order.reshape(1, -1))
    return res[None]


def solution(mesh):
    in_specs = (
        P("aux", None, None, None),
        P("aux", None),
        P("occ", None, None),
        P(),
        P("aux", None),
        P(),
    )
    return jax.shard_map(
        body, mesh=mesh, in_specs=in_specs, out_specs=P("aux", None, None), check_vma=False
    )
```

```python
import jax
import jax.numpy as jnp
from jax import lax
from jax.experimental import pallas as pl
from jax.experimental.pallas import tpu as pltpu
from jax.sharding import PartitionSpec as P

MESH = pl.DeviceIdType.MESH
F32 = jnp.float32
BF16 = jnp.bfloat16
I32 = jnp.int32
NY, NX, NC, NZ = 4, 4, 2, 8
NT, AB, SH, ORB, NSUP, NQ = 32, 8, 128, 16, 24, 16
JL = ORB // NC
PIECE = NSUP // (NX * NC)
LOADS = 8
PER_LOAD = NT // LOADS
ORDER, KEEP, NUS, MU, NU, LAST, FILLED, QQ, T0, T1, V0, V1, POS = 0, 1, 2, 3, 4, 5, 6, 7, 8, 9, 10, 11, 16
BATCHES = ((0, 1, 2), (0, 3, 1), (1, 0, 4))
GROUPS = ((0, 1, 2, 7), (3, 4, 5, 6))


def fill_tables(sbv, suv, bov, tabv):
    t = lax.broadcasted_iota(I32, (NT, NT), 0)
    lane = lax.broadcasted_iota(I32, (NT, NT), 1)

    def down(mask, value):
        return jnp.sum(jnp.where(mask, value, 0), axis=0, keepdims=True)

    def across(mask, value=1):
        return jnp.sum(jnp.where(mask, value, 0), axis=1, keepdims=True)

    diagonal, before = t == lane, lane < t
    mu_r, nu_r, q_r = [sbv[i : i + 1, :] for i in range(3)]
    mu, nu, q = [across(diagonal, v) for v in (mu_r, nu_r, q_r)]
    rank = across((q_r < q) | ((q_r == q) & before))
    follows = across((q_r == q) & before)
    second = across((mu_r == mu) & before)
    placed = rank == lane
    here = bov[...] == mu
    one, two = here & (second == 0), here & (second > 0)
    rows = {
        ORDER: down(placed, t),
        KEEP: down(placed & (follows > 0), 1),
        NUS: down(placed, jnp.broadcast_to(nu, (NT, NT))),
        MU: mu_r,
        NU: nu_r,
        LAST: jnp.maximum(down(q <= lane, 1) - 1, 0),
        FILLED: jnp.minimum(down(q == lane, 1), 1),
        QQ: q_r,
        T0: jnp.max(jnp.where(one, t, 0), axis=0, keepdims=True),
        T1: jnp.max(jnp.where(two, t, 0), axis=0, keepdims=True),
        V0: down(one, 1),
        V1: down(two, 1),
    }
    for i, v in rows.items():
        tabv[i : i + 1, 0:NT] = v
    block = lax.broadcasted_iota(I32, (NZ, 32), 1)
    pos = jnp.full((NZ, 32), NSUP, I32)
    for s in range(NSUP):
        pos = jnp.where(jnp.broadcast_to(suv[:, s : s + 1], (NZ, 32)) == block, s, pos)
    tabv[POS : POS + NZ, 0:32] = pos


def kernel(
    ints, coeff, metric, sb, support, border, out,
    cin, sbv, suv, bov, tabv, tabr, stab,
    iv, calla, callb, cown, c32, bst, bp, bsend, bps, rbuf, nat, tra, natt, trat, mg0, mg1, fo, fsend, fgot,
    fxs, fxr, ta, ft, bfull, gt, gs, gr, gx, gin, zall,
    in_sem, int_sem, tab_sem, zc_s, zc_r, xc_s, xc_r, cc_s, cc_r, ms_s, ms_r, mf_s, mf_r,
    ex_s, ex_r, mg_s, mg_r, fa_s, fa_r, fx_s, fx_r, gx_s, gx_r, z_s, z_r,
):
    d = lax.axis_index("aux")
    z = lax.axis_index("occ")
    y, x, c = d // (NX * NC), (d // NC) % NX, d % NC
    ys, xs, zs = [[lax.rem(v + k, n) for k in range(n)] for v, n in ((y, NY), (x, NX), (z, NZ))]

    def dev(yy, xx, cc, zz):
        return (yy * (NX * NC) + xx * NC + cc, zz)

    sibling = dev(y, x, 1 - c, z)

    def zpeer(k):
        return dev(y, x, c, zs[k])

    def xpeer(k):
        return dev(y, xs[k], c, z)

    def ypeer(k):
        return dev(ys[k], x, c, z)

    def plane(k):
        return ys[k // NX], xs[k % NX]

    def copy(src, dst, s, r, to):
        return pltpu.make_async_remote_copy(
            src_ref=src, dst_ref=dst, send_sem=s, recv_sem=r, device_id=to, device_id_type=MESH
        )

    pending = []

    def start(cp):
        cp.start()
        pending.append(cp)
        return cp

    def load(i):
        part = pl.ds(i * PER_LOAD, PER_LOAD)
        return pltpu.make_async_copy(ints.at[part], iv.at[part], int_sem.at[i])

    small = [
        pltpu.make_async_copy(src, dst, in_sem.at[i])
        for i, (src, dst) in enumerate(((coeff, cin), (sb, sbv), (support, suv), (border, bov)))
    ]
    for cp in small:
        cp.start()
    barrier = pltpu.get_barrier_semaphore()
    partners = [zpeer(k) for k in (4, 3, 5, 2, 6, 1, 7)]
    partners += [dev(*plane(k), c, z) for k in range(1, NX * NY)]
    partners += [sibling]
    partners += [dev(y, xs[k], 1 - c, z) for k in (1, 2, 3)]
    partners += [dev(ys[k], x, 1 - c, z) for k in (1, 2, 3)]
    for who in partners:
        pl.semaphore_signal(barrier, inc=1, device_id=who, device_id_type=MESH)
    for i in range(LOADS):
        load(i).start()

    def metric_part(h, k, m):
        if h == 0:
            col = (ys[k] * NX + m) * 256 + c * 128
        else:
            col = (m * NX + xs[k]) * 256 + (1 - c) * 128
        return metric.at[:, pl.ds(pl.multiple_of(col, 128), 128)]

    quarters = ((nat, ys, ypeer), (tra, xs, xpeer))
    for h, (buf, me, to) in enumerate(quarters):
        for m in range(4):
            pltpu.make_async_copy(metric_part(h, 0, m), buf.at[c, me[0], m], in_sem.at[4 + h]).start()

    small[0].wait()
    for i in range(ORB):
        c32[pl.ds(i, NSUP, stride=ORB), :] = cin[i].astype(F32)
    cown[:NSUP] = c32[...].astype(BF16).reshape(NSUP, ORB, SH)
    cown[NSUP] = jnp.zeros((ORB, SH), BF16)
    calla[0] = cown[...]
    for k in range(NZ // 2):
        calla[k, NSUP] = jnp.zeros((ORB, SH), BF16)
        callb[k, NSUP] = jnp.zeros((ORB, SH), BF16)
    tabv[...] = jnp.zeros(tabv.shape, I32)
    for cp in small[1:]:
        cp.wait()

    pl.semaphore_wait(barrier, len(partners))

    place = [xs[k] * (1 - c) + ys[k] * c for k in range(4)]
    place_n = [xs[k] * c + ys[k] * (1 - c) for k in range(4)]

    calls = (calla, callb)

    def spot(r):
        g = int(r in GROUPS[1])
        return calls[g].at[GROUPS[g].index(r)]

    def batch(b, part):
        g, lo, n = BATCHES[b]
        return calls[g].at[pl.ds(lo, n), part]

    def piece(k):
        return pl.ds(c * (NSUP // NC) + PIECE * place[(4 - k) % 4], PIECE)

    def piece_n(k):
        return pl.ds((1 - c) * (NSUP // NC) + PIECE * place_n[(4 - k) % 4], PIECE)

    def qpeer(k):
        return dev(ys[k] * c + y * (1 - c), xs[k] * (1 - c) + x * c, c, z)

    for k in (7, 1, 6, 4, 3, 5, 2):
        start(copy(cown.at[piece(0)], spot(NZ - k).at[piece(0)], zc_s.at[k - 1], zc_r.at[k - 1], zpeer(k)))
    for k in (2, 1, 3):
        for h, (buf, me, to) in enumerate(quarters):
            for m in range(4):
                part = buf.at[c, me[0], m]
                copy(metric_part(h, k, m), part, ms_s.at[h, k - 1], ms_r.at[h, k - 1], to(k)).start()
            part = buf.at[c, me[0]]
            pending.append(copy(part, part, ms_s.at[h, k - 1], ms_r.at[h, k - 1], to(k)))

    fill_tables(sbv, suv, bov, tabv)
    own_tab = pltpu.make_async_copy(tabv, stab.at[0], tab_sem.at[0])
    own_tab.start()
    tab_send = start(copy(tabv, tabr, ex_s.at[0], ex_r.at[0], sibling))
    own_tab.wait()

    zr = zs

    def entry(r, b):
        return stab[0, POS + zr[r], b]

    def half_transform(t, st):
        own = cown[entry(0, stab[0, MU, t])]
        rhs = jnp.concatenate([iv[t, a] for a in range(AB)], axis=1)
        res = jnp.dot(own, rhs, preferred_element_type=F32)
        for a in range(AB):
            bst[st, pl.ds(a, ORB, stride=AB), :] = res[:, a * SH : (a + 1) * SH]
        bp[t] = bst[st].astype(BF16)

    def half_loads(lo, hi):
        @pl.loop(lo, hi)
        def _(i):
            load(i).wait()
            for u in range(PER_LOAD):
                half_transform(i * PER_LOAD + u, u)

    def zwait(r):
        got = spot(r).at[piece(0)]
        copy(got, got, zc_s.at[NZ - r - 1], zc_r.at[NZ - r - 1], sibling).wait_recv()

    def spread(b):
        part = batch(b, piece(0))
        for k in (2, 1, 3):
            start(copy(part, part, xc_s.at[k - 1, b], xc_r.at[k - 1, b], qpeer(k)))
        start(copy(part, part, cc_s.at[0, b], cc_r.at[0, b], sibling))

    def relay(k, b):
        part = batch(b, piece(k))
        copy(part, part, xc_s.at[k - 1, b], xc_r.at[k - 1, b], sibling).wait_recv()
        start(copy(part, part, cc_s.at[k, b], cc_r.at[k, b], sibling))

    half_loads(0, LOADS // 2)
    zwait(7)
    spread(1)
    zwait(1)
    zwait(2)
    spread(0)
    half_loads(LOADS // 2, LOADS)

    rows_c = pl.ds(pl.multiple_of(c * 64, 64), 64)
    rows_n = pl.ds(pl.multiple_of((1 - c) * 64, 64), 64)

    @pl.loop(0, NT, unroll=4)
    def _(k):
        bsend[k] = bp[stab[0, ORDER, k], rows_n, :]

    b_send = start(copy(bsend, bps.at[1], ex_s.at[1], ex_r.at[1], sibling))

    @pl.loop(0, NT, unroll=4)
    def _(k):
        bps[0, k] = bp[stab[0, ORDER, k], rows_c, :]

    for r in (6, 3, 5, 4):
        zwait(r)
    spread(2)

    def got_panel(b):
        for k in (0, 1, 3, 2):
            part = batch(b, piece_n(k))
            copy(part, part, cc_s.at[k, b], cc_r.at[k, b], sibling).wait_recv()

    mfs = []
    for h, (buf, me, to) in enumerate(quarters):
        pltpu.make_async_copy(buf.at[c, me[0]], buf.at[c, me[0]], in_sem.at[4 + h]).wait()
        for k in (1, 3, 2):
            part = buf.at[c, me[4 - k]]
            copy(part, part, ms_s.at[h, k - 1], ms_r.at[h, k - 1], sibling).wait_recv()
        mfs.append(start(copy(buf.at[c], buf.at[c], mf_s.at[h], mf_r.at[h], sibling)))

    def transpose_quarters(cc):
        @pl.loop(0, 4)
        def _(i):
            for j in range(4):
                natt[cc, j, i] = nat[cc, i, j].T
                trat[cc, j, i] = tra[cc, i, j].T

    tab_send.wait_recv()
    sib_tab = pltpu.make_async_copy(tabr, stab.at[1], tab_sem.at[1])
    sib_tab.start()
    sib_tab.wait()
    for b in (1, 0):
        for k in (1, 3, 2):
            relay(k, b)
    transpose_quarters(c)
    for b in (1, 0):
        got_panel(b)

    def pick(flag, value):
        return jnp.where(jnp.full(value.shape, flag, I32) == 1, value, 0.0)

    def panel(b, groups):
        return jnp.concatenate([calls[g][i, entry(GROUPS[g][i], b)] for g in groups for i in range(4)], axis=0)

    nt = (((1,), (1,)), ((), ()))

    def m_rows(s):
        base = (c if s == 0 else 1 - c) * 128
        return pl.ds(pl.multiple_of(base, 128), 128)

    def m_part(h, me, j, s):
        return (mg0, mg1)[h].at[me, pl.ds(2 * j, 2), m_rows(s)]

    def ring(h):
        return (ys, ypeer) if h == 0 else (xs, xpeer)

    def m_copy(h, k, j, s):
        me, to = ring(h)
        part = m_part(h, me[0], j, s)
        return copy(part, part, mg_s.at[h, k - 1, j, s], mg_r.at[h, k - 1, j, s], to(k))

    def m_wait(h, j):
        me, to = ring(h)
        for s in range(NC):
            for k in (1, 3, 2):
                part = m_part(h, me[4 - k], j, s)
                copy(part, part, mg_s.at[h, k - 1, j, s], mg_r.at[h, k - 1, j, s], sibling).wait_recv()

    def m_send(j, s):
        for k in (2, 1, 3):
            for h in range(2):
                start(m_copy(h, k, j, s))

    def m_terms(g, s):
        rbuf[s, 0] = jnp.zeros((32, SH), F32)

        @pl.loop(0, NT, unroll=8)
        def _(k):
            part = panel(stab[s, NUS, k], (g,))
            none = jnp.zeros_like(part)
            rhs = [jnp.concatenate([part, none], axis=1), jnp.concatenate([none, part], axis=1)]
            lhs = jnp.concatenate([bps[s, k, :32], bps[s, k, 32:]], axis=1)
            term = lax.dot_general(lhs, jnp.concatenate(rhs, axis=0), nt, preferred_element_type=F32)
            rbuf[s, k + 1] = term + pick(stab[s, KEEP, k], rbuf[s, k])

        for h in range(NQ // 2):
            got = []
            for u in range(2):
                blk = rbuf[s, stab[s, LAST, 2 * h + u] + 1]
                got.append(pick(stab[s, FILLED, 2 * h + u], blk).reshape(4, AB, SH))
            both = jnp.concatenate(got, axis=1).astype(BF16)
            rows = pl.ds(pl.multiple_of((c if s == 0 else 1 - c) * 128 + h * 16, 16), 16)
            mg0[y, 2 * g : 2 * g + 2, rows, :] = both[:2]
            mg1[x, 2 * g : 2 * g + 2, rows, :] = both[2:]
        m_send(g, s)

    m_terms(0, 0)
    for k in (1, 3, 2):
        relay(k, 2)
    b_send.wait_recv()
    m_terms(0, 1)
    got_panel(2)

    def full_blocks(lo, hi):
        @pl.loop(lo, hi)
        def _(t):
            rhs = iv[t].reshape(AB * SH, SH)
            blk = lax.dot_general(panel(stab[0, NU, t], (0, 1)), rhs, nt, preferred_element_type=F32).astype(BF16)
            for a in range(AB):
                bfull[t, pl.ds(a * SH, SH), :] = blk[:, a * SH : (a + 1) * SH]

    def fit(h, j):
        got = (mg0, mg1)[h]
        rhs = [jnp.concatenate([got[m, 2 * j], got[m, 2 * j + 1]], axis=1) for m in range(4)]
        rhs = jnp.concatenate(rhs, axis=0)
        same, cross = ((natt, tra), (nat, trat))[h]
        if h == 0:
            lhs = [
                [(same if cr == ck else cross)[cr, r, k] for k in range(4) for ck in range(NC)]
                for r in range(4)
                for cr in range(NC)
            ]
        else:
            lhs = [
                [(same if cr == ck else cross)[ck, r, k] for k in range(4) for ck in range(NC)]
                for r in range(4)
                for cr in range(NC)
            ]
        lhs = jnp.concatenate([jnp.concatenate(v, axis=1) for v in lhs], axis=0)
        res = jnp.dot(lhs, rhs, preferred_element_type=F32)
        for r in range(4):
            fo[h, j, r, 0] = res[r * 256 : (r + 1) * 256, :SH]
            fo[h, j, r, 1] = res[r * 256 : (r + 1) * 256, SH:]

    def f_part(h, j, off):
        return fo.at[h, j, (xs, ys)[h][off]]

    def f_copy(h, j, k, cc):
        src = fsend.at[h, j, k - 1, :, pl.ds(cc * 128, 128)]
        to = dev(y, xs[k], cc, z) if h == 0 else dev(ys[k], x, cc, z)
        return copy(src, fgot.at[c, k - 1, h, j], fa_s.at[h, j, k - 1, cc], fa_r.at[h, j, k - 1, c], to)

    def fx(h, j):
        return copy(fxs.at[h, j], fxr.at[h, j], fx_s.at[h, j], fx_r.at[h, j], sibling)

    own_rows = pl.ds(pl.multiple_of(c * 128, 128), 128)
    sib_rows = pl.ds(pl.multiple_of((1 - c) * 128, 128), 128)

    def fits(j):
        for h in range(2):
            m_wait(h, j)
            fit(h, j)
            for k in (2, 1, 3):
                fsend[h, j, k - 1] = f_part(h, j, k)[...].astype(BF16)
                for cc in range(NC):
                    start(f_copy(h, j, k, cc))
            fxs[h, j] = f_part(h, j, 0)[:, sib_rows].astype(BF16)
            start(fx(h, j))

    def got_from(cs, h, j, u):
        total = f_part(h, j, 0)[u, own_rows] if cs is c else fxr[h, j, u].astype(F32)
        for k in range(3):
            total = total + fgot[cs, k, h, j, u].astype(F32)
        return total

    def totals(j):
        left = lax.broadcasted_iota(I32, (128, SH), 1) < 64
        for h in range(2):
            fx(h, j).wait_recv()
            for k in (1, 3, 2):
                for cc in range(NC):
                    part = fgot.at[cc, k - 1, h, j]
                    copy(part, part, fa_s.at[h, j, k - 1, cc], fa_r.at[h, j, k - 1, cc], sibling).wait_recv()
            for u in range(2):
                for w, cs in enumerate((c, 1 - c)):
                    val = got_from(cs, h, j, u)
                    if j == 0:
                        ta[w, 2 * h + u] = val
                    else:
                        old = ta[w, 2 * h + u]
                        row = JL * w + 2 * h + u
                        ft[pl.ds(row, 128, stride=ORB), :] = jnp.where(left, old, pltpu.roll(val, 64, axis=1))
                        ft[pl.ds(row + 4, 128, stride=ORB), :] = jnp.where(left, pltpu.roll(old, 64, axis=1), val)

    m_terms(1, 0)
    m_terms(1, 1)
    for cp in mfs:
        cp.wait_recv()
    transpose_quarters(1 - c)
    full_blocks(0, 10)
    fits(0)
    full_blocks(10, 24)
    fits(1)
    full_blocks(24, NT)
    totals(0)
    totals(1)

    ftq = ft.reshape(NQ, AB * ORB, SH)
    low = pl.ds(pl.multiple_of(c * JL, JL), JL)
    high = pl.ds(pl.multiple_of((1 - c) * JL, JL), JL)

    @pl.loop(0, NT, unroll=8)
    def _(t):
        rows = ftq[stab[0, QQ, t]]
        lhs = jnp.concatenate([rows[a * ORB : (a + 1) * ORB] for a in range(AB)], axis=1)
        res = jnp.dot(lhs.astype(BF16), bfull[t], preferred_element_type=F32)
        gt[t, low, :] = res[:JL]
        gt[t, high, :] = res[JL:]

    for s in range(32):
        one = pick(stab[0, V0, s], gt[stab[0, T0, s]])
        two = pick(stab[0, V1, s], gt[stab[0, T1, s]])
        gs[s % 2, s // 2] = one + two

    g_send = start(copy(gs.at[1 - c], gr, ex_s.at[4], ex_r.at[4], sibling))
    g_send.wait_recv()
    gx[...] = gs[c] + gr[...]
    for k in (10, 6, 14, 9, 11, 5, 7, 13, 15, 2, 8, 1, 3, 4, 12):
        yy, xx = plane(k)
        start(copy(gx.at[yy * NX + xx], gin.at[k], gx_s.at[k - 1], gx_r.at[k - 1], dev(yy, xx, c, z)))
    total = gx[y * NX + x]
    for k in (1, 3, 4, 12, 2, 8, 5, 7, 13, 15, 6, 14, 9, 11, 10):
        copy(gx.at[0], gin.at[k], gx_s.at[k - 1], gx_r.at[k - 1], sibling).wait_recv()
        total = total + gin[k]
    zall[z] = total
    for k in (4, 3, 5, 2, 6, 1, 7):
        start(copy(zall.at[z], zall.at[z], z_s.at[k - 1], z_r.at[k - 1], zpeer(k)))
    for k in (1, 7, 2, 6, 3, 5, 4):
        got = zall.at[zs[NZ - k]]
        copy(got, got, z_s.at[k - 1], z_r.at[k - 1], zpeer(k)).wait_recv()
    out[...] = zall[...].reshape(NZ * ORB, SH)

    for cp in pending:
        cp.wait_send()


def body(integrals, screened_blocks, coeff, support, metric, block_order):
    vm = pltpu.VMEM
    dma = pltpu.SemaphoreType.DMA
    any_spec = pl.BlockSpec(memory_space=pl.ANY)
    res = pl.pallas_call(
        kernel,
        out_shape=jax.ShapeDtypeStruct((SH, NZ * ORB), F32),
        in_specs=[any_spec] * 6,
        out_specs=pl.BlockSpec(memory_space=pltpu.VMEM),
        scratch_shapes=[
            vm((ORB, NSUP, SH), BF16),
            vm((3, NT), I32),
            vm((NZ, NSUP), I32),
            vm((1, 32), I32),
            vm((24, 128), I32),
            vm((24, 128), I32),
            pltpu.SMEM((2, 24, 128), I32),
            vm((NT, AB, SH, SH), BF16),
            vm((NZ // 2, NSUP + 1, ORB, SH), BF16),
            vm((NZ // 2, NSUP + 1, ORB, SH), BF16),
            vm((NSUP + 1, ORB, SH), BF16),
            vm((NSUP * ORB, SH), F32),
            vm((PER_LOAD, 128, SH), F32),
            vm((NT, 128, SH), BF16),
            vm((NT, 64, SH), BF16),
            vm((NC, NT, 64, SH), BF16),
            vm((NC, NT + 1, 32, SH), F32),
            vm((NC, 4, 4, 128, 128), BF16),
            vm((NC, 4, 4, 128, 128), BF16),
            vm((NC, 4, 4, 128, 128), BF16),
            vm((NC, 4, 4, 128, 128), BF16),
            vm((4, 4, 256, SH), BF16),
            vm((4, 4, 256, SH), BF16),
            vm((2, 2, 4, 2, 256, SH), F32),
            vm((2, 2, 3, 2, 256, SH), BF16),
            vm((NC, 3, 2, 2, 2, 128, SH), BF16),
            vm((2, 2, 2, 128, SH), BF16),
            vm((2, 2, 2, 128, SH), BF16),
            vm((2, 4, 128, SH), F32),
            vm((128 * ORB, SH), F32),
            vm((NT, AB * SH, SH), BF16),
            vm((NT, ORB, SH), F32),
            vm((NC, 16, ORB, SH), F32),
            vm((16, ORB, SH), F32),
            vm((16, ORB, SH), F32),
            vm((16, ORB, SH), F32),
            vm((NZ, ORB, SH), F32),
            dma((6,)), dma((LOADS,)), dma((2,)),
            dma((7,)), dma((7,)), dma((3, 3)), dma((3, 3)), dma((4, 3)), dma((4, 3)),
            dma((2, 3)), dma((2, 3)), dma((2,)), dma((2,)),
            dma((5,)), dma((5,)),
            dma((2, 3, 2, 2)), dma((2, 3, 2, 2)), dma((2, 2, 3, 2)), dma((2, 2, 3, 2)), dma((2, 2)), dma((2, 2)),
            dma((15,)), dma((15,)), dma((7,)), dma((7,)),
        ],
        compiler_params=pltpu.CompilerParams(
            collective_id=0, has_side_effects=True, vmem_limit_bytes=56 * 1024 * 1024
        ),
        cost_estimate=pl.CostEstimate(flops=4 * 10**9, bytes_accessed=10 * 10**6, transcendentals=0),
        name="exchange",
    )(integrals, coeff, metric, screened_blocks.T, support, block_order.reshape(1, -1))
    return res.T[None]


def solution(mesh):
    in_specs = (
        P("aux", None, None, None),
        P("aux", None),
        P("occ", None, None),
        P(),
        P("aux", None),
        P(),
    )
    return jax.shard_map(
        body, mesh=mesh, in_specs=in_specs, out_specs=P("aux", None, None), check_vma=False
    )
```

```python
import jax
import jax.numpy as jnp
from jax import lax
from jax.experimental import pallas as pl
from jax.experimental.pallas import tpu as pltpu
from jax.sharding import PartitionSpec as P

MESH = pl.DeviceIdType.MESH
F32 = jnp.float32
BF16 = jnp.bfloat16
I32 = jnp.int32
NY, NX, NC, NZ = 4, 4, 2, 8
NT, AB, SH, ORB, NSUP, NQ = 32, 8, 128, 16, 24, 16
JL = ORB // NC
PIECE = NSUP // (NX * NC)
LOADS = 8
PER_LOAD = NT // LOADS
ORDER, KEEP, NUS, MU, NU, LAST, FILLED, QQ, T0, T1, V0, V1, POS = 0, 1, 2, 3, 4, 5, 6, 7, 8, 9, 10, 11, 16
BATCHES = ((0, 1, 2), (0, 3, 1), (1, 0, 4))
GROUPS = ((0, 1, 2, 7), (3, 4, 5, 6))


def fill_tables(sbv, suv, bov, tabv):
    t = lax.broadcasted_iota(I32, (NT, NT), 0)
    lane = lax.broadcasted_iota(I32, (NT, NT), 1)

    def down(mask, value):
        return jnp.sum(jnp.where(mask, value, 0), axis=0, keepdims=True)

    def across(mask, value=1):
        return jnp.sum(jnp.where(mask, value, 0), axis=1, keepdims=True)

    diagonal, before = t == lane, lane < t
    mu_r, nu_r, q_r = [sbv[i : i + 1, :] for i in range(3)]
    mu, nu, q = [across(diagonal, v) for v in (mu_r, nu_r, q_r)]
    rank = across((q_r < q) | ((q_r == q) & before))
    follows = across((q_r == q) & before)
    second = across((mu_r == mu) & before)
    placed = rank == lane
    here = bov[...] == mu
    one, two = here & (second == 0), here & (second > 0)
    rows = {
        ORDER: down(placed, t),
        KEEP: down(placed & (follows > 0), 1),
        NUS: down(placed, jnp.broadcast_to(nu, (NT, NT))),
        MU: mu_r,
        NU: nu_r,
        LAST: jnp.maximum(down(q <= lane, 1) - 1, 0),
        FILLED: jnp.minimum(down(q == lane, 1), 1),
        QQ: q_r,
        T0: jnp.max(jnp.where(one, t, 0), axis=0, keepdims=True),
        T1: jnp.max(jnp.where(two, t, 0), axis=0, keepdims=True),
        V0: down(one, 1),
        V1: down(two, 1),
    }
    for i, v in rows.items():
        tabv[i : i + 1, 0:NT] = v
    block = lax.broadcasted_iota(I32, (NZ, 32), 1)
    pos = jnp.full((NZ, 32), NSUP, I32)
    for s in range(NSUP):
        pos = jnp.where(jnp.broadcast_to(suv[:, s : s + 1], (NZ, 32)) == block, s, pos)
    tabv[POS : POS + NZ, 0:32] = pos


def kernel(
    ints, coeff, metric, sb, support, border, out,
    cin, sbv, suv, bov, tabv, tabr, stab,
    iv, calla, callb, cown, c32, bst, bp, bsend, bps, rbuf, nat, tra, natt, trat, mg0, mg1, fo, fsend, fgot,
    fxs, fxr, ta, ft, bfull, gt, gs, gr, gx, gin, zall,
    in_sem, int_sem, tab_sem, zc_s, zc_r, xc_s, xc_r, cc_s, cc_r, ms_s, ms_r, mf_s, mf_r,
    ex_s, ex_r, mg_s, mg_r, fa_s, fa_r, fx_s, fx_r, gx_s, gx_r, z_s, z_r,
):
    d = lax.axis_index("aux")
    z = lax.axis_index("occ")
    y, x, c = d // (NX * NC), (d // NC) % NX, d % NC
    ys, xs, zs = [[lax.rem(v + k, n) for k in range(n)] for v, n in ((y, NY), (x, NX), (z, NZ))]

    def dev(yy, xx, cc, zz):
        return (yy * (NX * NC) + xx * NC + cc, zz)

    sibling = dev(y, x, 1 - c, z)

    def zpeer(k):
        return dev(y, x, c, zs[k])

    def xpeer(k):
        return dev(y, xs[k], c, z)

    def ypeer(k):
        return dev(ys[k], x, c, z)

    def plane(k):
        return ys[k // NX], xs[k % NX]

    def copy(src, dst, s, r, to):
        return pltpu.make_async_remote_copy(
            src_ref=src, dst_ref=dst, send_sem=s, recv_sem=r, device_id=to, device_id_type=MESH
        )

    pending = []

    def start(cp):
        cp.start()
        pending.append(cp)
        return cp

    def load(i):
        part = pl.ds(i * PER_LOAD, PER_LOAD)
        return pltpu.make_async_copy(ints.at[part], iv.at[part], int_sem.at[i])

    small = [
        pltpu.make_async_copy(src, dst, in_sem.at[i])
        for i, (src, dst) in enumerate(((coeff, cin), (sb, sbv), (support, suv), (border, bov)))
    ]
    for cp in small:
        cp.start()
    barrier = pltpu.get_barrier_semaphore()
    partners = [zpeer(k) for k in (4, 3, 5, 2, 6, 1, 7)]
    partners += [dev(*plane(k), c, z) for k in range(1, NX * NY)]
    partners += [sibling]
    partners += [dev(y, xs[k], 1 - c, z) for k in (1, 2, 3)]
    partners += [dev(ys[k], x, 1 - c, z) for k in (1, 2, 3)]
    for who in partners:
        pl.semaphore_signal(barrier, inc=1, device_id=who, device_id_type=MESH)
    for i in range(LOADS):
        load(i).start()

    def metric_part(h, k, m):
        if h == 0:
            col = (ys[k] * NX + m) * 256 + c * 128
        else:
            col = (m * NX + xs[k]) * 256 + (1 - c) * 128
        return metric.at[:, pl.ds(pl.multiple_of(col, 128), 128)]

    quarters = ((nat, ys, ypeer), (tra, xs, xpeer))
    for h, (buf, me, to) in enumerate(quarters):
        for m in range(4):
            pltpu.make_async_copy(metric_part(h, 0, m), buf.at[c, me[0], m], in_sem.at[4 + h]).start()

    small[0].wait()
    for i in range(ORB):
        c32[pl.ds(i, NSUP, stride=ORB), :] = cin[i].astype(F32)
    cown[:NSUP] = c32[...].astype(BF16).reshape(NSUP, ORB, SH)
    cown[NSUP] = jnp.zeros((ORB, SH), BF16)
    calla[0] = cown[...]
    for k in range(NZ // 2):
        calla[k, NSUP] = jnp.zeros((ORB, SH), BF16)
        callb[k, NSUP] = jnp.zeros((ORB, SH), BF16)
    tabv[...] = jnp.zeros(tabv.shape, I32)
    for cp in small[1:]:
        cp.wait()

    pl.semaphore_wait(barrier, len(partners))

    place = [xs[k] * (1 - c) + ys[k] * c for k in range(4)]
    place_n = [xs[k] * c + ys[k] * (1 - c) for k in range(4)]

    calls = (calla, callb)

    def spot(r):
        g = int(r in GROUPS[1])
        return calls[g].at[GROUPS[g].index(r)]

    def batch(b, part):
        g, lo, n = BATCHES[b]
        return calls[g].at[pl.ds(lo, n), part]

    def piece(k):
        return pl.ds(c * (NSUP // NC) + PIECE * place[(4 - k) % 4], PIECE)

    def piece_n(k):
        return pl.ds((1 - c) * (NSUP // NC) + PIECE * place_n[(4 - k) % 4], PIECE)

    def qpeer(k):
        return dev(ys[k] * c + y * (1 - c), xs[k] * (1 - c) + x * c, c, z)

    for k in (7, 1, 6, 4, 3, 5, 2):
        start(copy(cown.at[piece(0)], spot(NZ - k).at[piece(0)], zc_s.at[k - 1], zc_r.at[k - 1], zpeer(k)))
    def metric_send(k):
        for h, (buf, me, to) in enumerate(quarters):
            for m in range(4):
                part = buf.at[c, me[0], m]
                copy(metric_part(h, k, m), part, ms_s.at[h, k - 1], ms_r.at[h, k - 1], to(k)).start()
            part = buf.at[c, me[0]]
            pending.append(copy(part, part, ms_s.at[h, k - 1], ms_r.at[h, k - 1], to(k)))

    metric_send(1)
    metric_send(3)
    fill_tables(sbv, suv, bov, tabv)
    own_tab = pltpu.make_async_copy(tabv, stab.at[0], tab_sem.at[0])
    own_tab.start()
    tab_send = start(copy(tabv, tabr, ex_s.at[0], ex_r.at[0], sibling))
    own_tab.wait()

    zr = zs

    def entry(r, b):
        return stab[0, POS + zr[r], b]

    def half_transform(t, st):
        own = cown[entry(0, stab[0, MU, t])]
        rhs = jnp.concatenate([iv[t, a] for a in range(AB)], axis=1)
        res = jnp.dot(own, rhs, preferred_element_type=F32)
        for a in range(AB):
            bst[st, pl.ds(a, ORB, stride=AB), :] = res[:, a * SH : (a + 1) * SH]
        bp[t] = bst[st].astype(BF16)

    def half_loads(lo, hi):
        @pl.loop(lo, hi)
        def _(i):
            load(i).wait()
            for u in range(PER_LOAD):
                half_transform(i * PER_LOAD + u, u)

    def zwait(r):
        got = spot(r).at[piece(0)]
        copy(got, got, zc_s.at[NZ - r - 1], zc_r.at[NZ - r - 1], sibling).wait_recv()

    def spread(b):
        part = batch(b, piece(0))
        for k in (2, 1, 3):
            start(copy(part, part, xc_s.at[k - 1, b], xc_r.at[k - 1, b], qpeer(k)))
        start(copy(part, part, cc_s.at[0, b], cc_r.at[0, b], sibling))

    def relay(k, b):
        part = batch(b, piece(k))
        copy(part, part, xc_s.at[k - 1, b], xc_r.at[k - 1, b], sibling).wait_recv()
        start(copy(part, part, cc_s.at[k, b], cc_r.at[k, b], sibling))

    half_loads(0, LOADS // 2)
    zwait(7)
    spread(1)
    zwait(1)
    zwait(2)
    spread(0)
    metric_send(2)
    half_loads(LOADS // 2, LOADS)

    rows_c = pl.ds(pl.multiple_of(c * 64, 64), 64)
    rows_n = pl.ds(pl.multiple_of((1 - c) * 64, 64), 64)

    @pl.loop(0, NT, unroll=4)
    def _(k):
        bsend[k] = bp[stab[0, ORDER, k], rows_n, :]

    b_send = start(copy(bsend, bps.at[1], ex_s.at[1], ex_r.at[1], sibling))

    @pl.loop(0, NT, unroll=4)
    def _(k):
        bps[0, k] = bp[stab[0, ORDER, k], rows_c, :]

    for r in (6, 3, 5, 4):
        zwait(r)
    spread(2)

    def got_panel(b):
        for k in (0, 1, 3, 2):
            part = batch(b, piece_n(k))
            copy(part, part, cc_s.at[k, b], cc_r.at[k, b], sibling).wait_recv()

    def transpose_quarters(cc):
        @pl.loop(0, 4)
        def _(i):
            for j in range(4):
                natt[cc, j, i] = nat[cc, i, j].T
                trat[cc, j, i] = tra[cc, i, j].T

    tab_send.wait_recv()
    sib_tab = pltpu.make_async_copy(tabr, stab.at[1], tab_sem.at[1])
    sib_tab.start()
    sib_tab.wait()
    for b in (1, 0):
        for k in (1, 3, 2):
            relay(k, b)
    for b in (1, 0):
        got_panel(b)

    def pick(flag, value):
        return jnp.where(jnp.full(value.shape, flag, I32) == 1, value, 0.0)

    def panel(b, groups):
        return jnp.concatenate([calls[g][i, entry(GROUPS[g][i], b)] for g in groups for i in range(4)], axis=0)

    nt = (((1,), (1,)), ((), ()))

    def m_rows(s):
        base = (c if s == 0 else 1 - c) * 128
        return pl.ds(pl.multiple_of(base, 128), 128)

    def m_part(h, me, j, s):
        return (mg0, mg1)[h].at[me, pl.ds(2 * j, 2), m_rows(s)]

    def ring(h):
        return (ys, ypeer) if h == 0 else (xs, xpeer)

    def m_copy(h, k, j, s):
        me, to = ring(h)
        part = m_part(h, me[0], j, s)
        return copy(part, part, mg_s.at[h, k - 1, j, s], mg_r.at[h, k - 1, j, s], to(k))

    def m_wait(h, j, ks):
        me, to = ring(h)
        for s in range(NC):
            for k in ks:
                part = m_part(h, me[4 - k], j, s)
                copy(part, part, mg_s.at[h, k - 1, j, s], mg_r.at[h, k - 1, j, s], sibling).wait_recv()

    def m_send(j, s):
        for k in (2, 1, 3):
            for h in range(2):
                start(m_copy(h, k, j, s))

    def m_terms(g, s):
        rbuf[s, 0] = jnp.zeros((32, SH), F32)

        @pl.loop(0, NT, unroll=8)
        def _(k):
            part = panel(stab[s, NUS, k], (g,))
            term = lax.dot_general(bps[s, k], part, nt, preferred_element_type=F32)
            term = jnp.concatenate([term[:32], term[32:]], axis=1)
            rbuf[s, k + 1] = term + pick(stab[s, KEEP, k], rbuf[s, k])

        for h in range(NQ // 2):
            got = []
            for u in range(2):
                blk = rbuf[s, stab[s, LAST, 2 * h + u] + 1]
                got.append(pick(stab[s, FILLED, 2 * h + u], blk).reshape(4, AB, SH))
            both = jnp.concatenate(got, axis=1).astype(BF16)
            rows = pl.ds(pl.multiple_of((c if s == 0 else 1 - c) * 128 + h * 16, 16), 16)
            mg0[y, 2 * g : 2 * g + 2, rows, :] = both[:2]
            mg1[x, 2 * g : 2 * g + 2, rows, :] = both[2:]
        m_send(g, s)

    m_terms(0, 0)
    for k in (1, 3, 2):
        relay(k, 2)
    b_send.wait_recv()
    m_terms(0, 1)
    got_panel(2)

    def full_blocks(lo, hi):
        @pl.loop(lo, hi)
        def _(t):
            rhs = iv[t].reshape(AB * SH, SH)
            blk = lax.dot_general(panel(stab[0, NU, t], (0, 1)), rhs, nt, preferred_element_type=F32).astype(BF16)
            for a in range(AB):
                bfull[t, pl.ds(a * SH, SH), :] = blk[:, a * SH : (a + 1) * SH]

    def fit(h, j, near):
        got, me = (mg0, mg1)[h], (ys, xs)[h]
        blocks = [me[k] for k in ((0, 1, 3) if near else (2,))]
        rhs = [jnp.concatenate([got[m, 2 * j], got[m, 2 * j + 1]], axis=1) for m in blocks]
        same, cross = ((natt, tra), (nat, trat))[h]
        lhs = [
            [(same if cr == ck else cross)[(cr, ck)[h], r, m] for m in blocks for ck in range(NC)]
            for r in range(4)
            for cr in range(NC)
        ]
        lhs = jnp.concatenate([jnp.concatenate(v, axis=1) for v in lhs], axis=0)
        res = jnp.dot(lhs, jnp.concatenate(rhs, axis=0), preferred_element_type=F32)
        for r in range(4):
            for u in range(2):
                part = res[r * 256 : (r + 1) * 256, u * SH : (u + 1) * SH]
                fo[h, j, r, u] = part if near else fo[h, j, r, u] + part

    def f_part(h, j, off):
        return fo.at[h, j, (xs, ys)[h][off]]

    def f_copy(h, j, k, cc):
        src = fsend.at[h, j, k - 1, :, pl.ds(cc * 128, 128)]
        to = dev(y, xs[k], cc, z) if h == 0 else dev(ys[k], x, cc, z)
        return copy(src, fgot.at[c, k - 1, h, j], fa_s.at[h, j, k - 1, cc], fa_r.at[h, j, k - 1, c], to)

    def fx(h, j):
        return copy(fxs.at[h, j], fxr.at[h, j], fx_s.at[h, j], fx_r.at[h, j], sibling)

    own_rows = pl.ds(pl.multiple_of(c * 128, 128), 128)
    sib_rows = pl.ds(pl.multiple_of((1 - c) * 128, 128), 128)

    def fits(j):
        for h in range(2):
            m_wait(h, j, (1, 3))
            fit(h, j, True)
        for h in range(2):
            m_wait(h, j, (2,))
            fit(h, j, False)
            for k in (2, 1, 3):
                fsend[h, j, k - 1] = f_part(h, j, k)[...].astype(BF16)
                for cc in range(NC):
                    start(f_copy(h, j, k, cc))
            fxs[h, j] = f_part(h, j, 0)[:, sib_rows].astype(BF16)
            start(fx(h, j))

    def got_from(cs, h, j, u):
        total = f_part(h, j, 0)[u, own_rows] if cs is c else fxr[h, j, u].astype(F32)
        for k in range(3):
            total = total + fgot[cs, k, h, j, u].astype(F32)
        return total

    def totals(j):
        left = lax.broadcasted_iota(I32, (128, SH), 1) < 64
        for h in range(2):
            fx(h, j).wait_recv()
            for k in (1, 3, 2):
                for cc in range(NC):
                    part = fgot.at[cc, k - 1, h, j]
                    copy(part, part, fa_s.at[h, j, k - 1, cc], fa_r.at[h, j, k - 1, cc], sibling).wait_recv()
            for u in range(2):
                for w, cs in enumerate((c, 1 - c)):
                    val = got_from(cs, h, j, u)
                    if j == 0:
                        ta[w, 2 * h + u] = val
                    else:
                        old = ta[w, 2 * h + u]
                        row = JL * w + 2 * h + u
                        ft[pl.ds(row, 128, stride=ORB), :] = jnp.where(left, old, pltpu.roll(val, 64, axis=1))
                        ft[pl.ds(row + 4, 128, stride=ORB), :] = jnp.where(left, pltpu.roll(old, 64, axis=1), val)

    m_terms(1, 0)
    m_terms(1, 1)
    mfs = []
    for h, (buf, me, to) in enumerate(quarters):
        pltpu.make_async_copy(buf.at[c, me[0]], buf.at[c, me[0]], in_sem.at[4 + h]).wait()
        for k in (1, 3, 2):
            part = buf.at[c, me[4 - k]]
            copy(part, part, ms_s.at[h, k - 1], ms_r.at[h, k - 1], sibling).wait_recv()
        mfs.append(start(copy(buf.at[c], buf.at[c], mf_s.at[h], mf_r.at[h], sibling)))

    full_blocks(0, 4)
    transpose_quarters(c)
    for cp in mfs:
        cp.wait_recv()
    transpose_quarters(1 - c)
    full_blocks(4, 10)
    fits(0)
    full_blocks(10, 24)
    fits(1)
    full_blocks(24, NT)
    totals(0)
    totals(1)

    ftq = ft.reshape(NQ, AB * ORB, SH)
    low = pl.ds(pl.multiple_of(c * JL, JL), JL)
    high = pl.ds(pl.multiple_of((1 - c) * JL, JL), JL)

    @pl.loop(0, NT, unroll=8)
    def _(t):
        rows = ftq[stab[0, QQ, t]]
        lhs = jnp.concatenate([rows[a * ORB : (a + 1) * ORB] for a in range(AB)], axis=1)
        res = jnp.dot(lhs.astype(BF16), bfull[t], preferred_element_type=F32)
        gt[t, low, :] = res[:JL]
        gt[t, high, :] = res[JL:]

    for s in range(32):
        one = pick(stab[0, V0, s], gt[stab[0, T0, s]])
        two = pick(stab[0, V1, s], gt[stab[0, T1, s]])
        gs[s % 2, s // 2] = one + two

    g_send = start(copy(gs.at[1 - c], gr, ex_s.at[4], ex_r.at[4], sibling))
    g_send.wait_recv()
    gx[...] = gs[c] + gr[...]
    for k in (10, 6, 14, 9, 11, 5, 7, 13, 15, 2, 8, 1, 3, 4, 12):
        yy, xx = plane(k)
        start(copy(gx.at[yy * NX + xx], gin.at[k], gx_s.at[k - 1], gx_r.at[k - 1], dev(yy, xx, c, z)))
    total = gx[y * NX + x]
    for k in (1, 3, 4, 12, 2, 8, 5, 7, 13, 15, 6, 14, 9, 11, 10):
        copy(gx.at[0], gin.at[k], gx_s.at[k - 1], gx_r.at[k - 1], sibling).wait_recv()
        total = total + gin[k]
    zall[z] = total
    for k in (4, 3, 5, 2, 6, 1, 7):
        start(copy(zall.at[z], zall.at[z], z_s.at[k - 1], z_r.at[k - 1], zpeer(k)))
    for k in (1, 7, 2, 6, 3, 5, 4):
        got = zall.at[zs[NZ - k]]
        copy(got, got, z_s.at[k - 1], z_r.at[k - 1], zpeer(k)).wait_recv()
    whole = zall[...].reshape(NZ * ORB, SH).T
    even = lax.rem(lax.broadcasted_iota(I32, whole.shape, 0), 2) == 0
    out[0] = jnp.where(even, whole, 0.0)
    out[1] = jnp.where(even, 0.0, whole)

    for cp in pending:
        cp.wait_send()


def body(integrals, screened_blocks, coeff, support, metric, block_order):
    vm = pltpu.VMEM
    dma = pltpu.SemaphoreType.DMA
    any_spec = pl.BlockSpec(memory_space=pl.ANY)
    res = pl.pallas_call(
        kernel,
        out_shape=jax.ShapeDtypeStruct((2, SH, NZ * ORB), F32),
        in_specs=[any_spec] * 6,
        out_specs=pl.BlockSpec(memory_space=pltpu.VMEM),
        scratch_shapes=[
            vm((ORB, NSUP, SH), BF16),
            vm((3, NT), I32),
            vm((NZ, NSUP), I32),
            vm((1, 32), I32),
            vm((24, 128), I32),
            vm((24, 128), I32),
            pltpu.SMEM((2, 24, 128), I32),
            vm((NT, AB, SH, SH), BF16),
            vm((NZ // 2, NSUP + 1, ORB, SH), BF16),
            vm((NZ // 2, NSUP + 1, ORB, SH), BF16),
            vm((NSUP + 1, ORB, SH), BF16),
            vm((NSUP * ORB, SH), F32),
            vm((PER_LOAD, 128, SH), F32),
            vm((NT, 128, SH), BF16),
            vm((NT, 64, SH), BF16),
            vm((NC, NT, 64, SH), BF16),
            vm((NC, NT + 1, 32, SH), F32),
            vm((NC, 4, 4, 128, 128), BF16),
            vm((NC, 4, 4, 128, 128), BF16),
            vm((NC, 4, 4, 128, 128), BF16),
            vm((NC, 4, 4, 128, 128), BF16),
            vm((4, 4, 256, SH), BF16),
            vm((4, 4, 256, SH), BF16),
            vm((2, 2, 4, 2, 256, SH), F32),
            vm((2, 2, 3, 2, 256, SH), BF16),
            vm((NC, 3, 2, 2, 2, 128, SH), BF16),
            vm((2, 2, 2, 128, SH), BF16),
            vm((2, 2, 2, 128, SH), BF16),
            vm((2, 4, 128, SH), F32),
            vm((128 * ORB, SH), F32),
            vm((NT, AB * SH, SH), BF16),
            vm((NT, ORB, SH), F32),
            vm((NC, 16, ORB, SH), F32),
            vm((16, ORB, SH), F32),
            vm((16, ORB, SH), F32),
            vm((16, ORB, SH), F32),
            vm((NZ, ORB, SH), F32),
            dma((6,)), dma((LOADS,)), dma((2,)),
            dma((7,)), dma((7,)), dma((3, 3)), dma((3, 3)), dma((4, 3)), dma((4, 3)),
            dma((2, 3)), dma((2, 3)), dma((2,)), dma((2,)),
            dma((5,)), dma((5,)),
            dma((2, 3, 2, 2)), dma((2, 3, 2, 2)), dma((2, 2, 3, 2)), dma((2, 2, 3, 2)), dma((2, 2)), dma((2, 2)),
            dma((15,)), dma((15,)), dma((7,)), dma((7,)),
        ],
        compiler_params=pltpu.CompilerParams(
            collective_id=0, has_side_effects=True, vmem_limit_bytes=56 * 1024 * 1024
        ),
        cost_estimate=pl.CostEstimate(flops=4 * 10**9, bytes_accessed=10 * 10**6, transcendentals=0),
        name="exchange",
    )(integrals, coeff, metric, screened_blocks.T, support, block_order.reshape(1, -1))
    return (res[0] + res[1])[None]


def solution(mesh):
    in_specs = (
        P("aux", None, None, None),
        P("aux", None),
        P("occ", None, None),
        P(),
        P("aux", None),
        P(),
    )
    return jax.shard_map(
        body, mesh=mesh, in_specs=in_specs, out_specs=P("aux", None, None), check_vma=False
    )
```

```python
import jax
import jax.numpy as jnp
from jax import lax
from jax.experimental import pallas as pl
from jax.experimental.pallas import tpu as pltpu
from jax.sharding import PartitionSpec as P

MESH = pl.DeviceIdType.MESH
F32 = jnp.float32
BF16 = jnp.bfloat16
I32 = jnp.int32
NY, NX, NC, NZ = 4, 4, 2, 8
NT, AB, SH, ORB, NSUP, NQ = 32, 8, 128, 16, 24, 16
JL = ORB // NC
PIECE = NSUP // (NX * NC)
LOADS = 8
PER_LOAD = NT // LOADS
ORDER, KEEP, NUS, MU, NU, LAST, FILLED, QQ, T0, T1, V0, V1, POS = 0, 1, 2, 3, 4, 5, 6, 7, 8, 9, 10, 11, 16
BATCHES = ((0, 1, 2), (0, 3, 1), (1, 0, 4))
GROUPS = ((0, 1, 2, 7), (3, 4, 5, 6))


def fill_tables(sbv, suv, bov, tabv):
    t = lax.broadcasted_iota(I32, (NT, NT), 0)
    lane = lax.broadcasted_iota(I32, (NT, NT), 1)

    def down(mask, value):
        return jnp.sum(jnp.where(mask, value, 0), axis=0, keepdims=True)

    def across(mask, value=1):
        return jnp.sum(jnp.where(mask, value, 0), axis=1, keepdims=True)

    diagonal, before = t == lane, lane < t
    mu_r, nu_r, q_r = [sbv[i : i + 1, :] for i in range(3)]
    mu, nu, q = [across(diagonal, v) for v in (mu_r, nu_r, q_r)]
    rank = across((q_r < q) | ((q_r == q) & before))
    follows = across((q_r == q) & before)
    second = across((mu_r == mu) & before)
    placed = rank == lane
    here = bov[...] == mu
    one, two = here & (second == 0), here & (second > 0)
    rows = {
        ORDER: down(placed, t),
        KEEP: down(placed & (follows > 0), 1),
        NUS: down(placed, jnp.broadcast_to(nu, (NT, NT))),
        MU: mu_r,
        NU: nu_r,
        LAST: jnp.maximum(down(q <= lane, 1) - 1, 0),
        FILLED: jnp.minimum(down(q == lane, 1), 1),
        QQ: q_r,
        T0: jnp.max(jnp.where(one, t, 0), axis=0, keepdims=True),
        T1: jnp.max(jnp.where(two, t, 0), axis=0, keepdims=True),
        V0: down(one, 1),
        V1: down(two, 1),
    }
    for i, v in rows.items():
        tabv[i : i + 1, 0:NT] = v
    block = lax.broadcasted_iota(I32, (NZ, 32), 1)
    pos = jnp.full((NZ, 32), NSUP, I32)
    for s in range(NSUP):
        pos = jnp.where(jnp.broadcast_to(suv[:, s : s + 1], (NZ, 32)) == block, s, pos)
    tabv[POS : POS + NZ, 0:32] = pos


def kernel(
    ints, coeff, metric, sb, support, border, out,
    cin, sbv, suv, bov, tabv, tabr, stab,
    iv, calla, callb, cown, c32, bst, bp, bsend, bps, rbuf, nat, tra, natt, trat, mg0, mg1, fo, fsend, fgot,
    fxs, fxr, ta, ft, bfull, gt, gs, gr, gx, gin, zall,
    in_sem, int_sem, tab_sem, zc_s, zc_r, xc_s, xc_r, cc_s, cc_r, ms_s, ms_r, mf_s, mf_r,
    ex_s, ex_r, mg_s, mg_r, fa_s, fa_r, fx_s, fx_r, gx_s, gx_r, z_s, z_r,
):
    d = lax.axis_index("aux")
    z = lax.axis_index("occ")
    y, x, c = d // (NX * NC), (d // NC) % NX, d % NC
    ys, xs, zs = [[lax.rem(v + k, n) for k in range(n)] for v, n in ((y, NY), (x, NX), (z, NZ))]

    def dev(yy, xx, cc, zz):
        return (yy * (NX * NC) + xx * NC + cc, zz)

    sibling = dev(y, x, 1 - c, z)

    def zpeer(k):
        return dev(y, x, c, zs[k])

    def xpeer(k):
        return dev(y, xs[k], c, z)

    def ypeer(k):
        return dev(ys[k], x, c, z)

    def plane(k):
        return ys[k // NX], xs[k % NX]

    def copy(src, dst, s, r, to):
        return pltpu.make_async_remote_copy(
            src_ref=src, dst_ref=dst, send_sem=s, recv_sem=r, device_id=to, device_id_type=MESH
        )

    pending = []

    def start(cp):
        cp.start()
        pending.append(cp)
        return cp

    def drain(lo, hi):
        for cp in pending[lo:hi]:
            cp.wait_send()

    def load(i):
        part = pl.ds(i * PER_LOAD, PER_LOAD)
        return pltpu.make_async_copy(ints.at[part], iv.at[part], int_sem.at[i])

    small = [
        pltpu.make_async_copy(src, dst, in_sem.at[i])
        for i, (src, dst) in enumerate(((coeff, cin), (sb, sbv), (support, suv), (border, bov)))
    ]
    for cp in small:
        cp.start()
    barrier = pltpu.get_barrier_semaphore()
    partners = [zpeer(k) for k in (4, 3, 5, 2, 6, 1, 7)]
    partners += [dev(*plane(k), c, z) for k in range(1, NX * NY)]
    partners += [sibling]
    partners += [dev(y, xs[k], 1 - c, z) for k in (1, 2, 3)]
    partners += [dev(ys[k], x, 1 - c, z) for k in (1, 2, 3)]
    for who in partners:
        pl.semaphore_signal(barrier, inc=1, device_id=who, device_id_type=MESH)
    for i in range(LOADS):
        load(i).start()

    def metric_part(h, k, m):
        if h == 0:
            col = (ys[k] * NX + m) * 256 + c * 128
        else:
            col = (m * NX + xs[k]) * 256 + (1 - c) * 128
        return metric.at[:, pl.ds(pl.multiple_of(col, 128), 128)]

    quarters = ((nat, ys, ypeer), (tra, xs, xpeer))
    for h, (buf, me, to) in enumerate(quarters):
        for m in range(4):
            pltpu.make_async_copy(metric_part(h, 0, m), buf.at[c, me[0], m], in_sem.at[4 + h]).start()

    small[0].wait()
    for i in range(ORB):
        c32[pl.ds(i, NSUP, stride=ORB), :] = cin[i].astype(F32)
    cown[:NSUP] = c32[...].astype(BF16).reshape(NSUP, ORB, SH)
    cown[NSUP] = jnp.zeros((ORB, SH), BF16)
    calla[0] = cown[...]
    for k in range(NZ // 2):
        calla[k, NSUP] = jnp.zeros((ORB, SH), BF16)
        callb[k, NSUP] = jnp.zeros((ORB, SH), BF16)
    tabv[...] = jnp.zeros(tabv.shape, I32)
    for cp in small[1:]:
        cp.wait()

    pl.semaphore_wait(barrier, len(partners))

    place = [xs[k] * (1 - c) + ys[k] * c for k in range(4)]
    place_n = [xs[k] * c + ys[k] * (1 - c) for k in range(4)]

    calls = (calla, callb)

    def spot(r):
        g = int(r in GROUPS[1])
        return calls[g].at[GROUPS[g].index(r)]

    def batch(b, part):
        g, lo, n = BATCHES[b]
        return calls[g].at[pl.ds(lo, n), part]

    def piece(k):
        return pl.ds(c * (NSUP // NC) + PIECE * place[(4 - k) % 4], PIECE)

    def piece_n(k):
        return pl.ds((1 - c) * (NSUP // NC) + PIECE * place_n[(4 - k) % 4], PIECE)

    def qpeer(k):
        return dev(ys[k] * c + y * (1 - c), xs[k] * (1 - c) + x * c, c, z)

    for k in (7, 1, 6, 4, 3, 5, 2):
        start(copy(cown.at[piece(0)], spot(NZ - k).at[piece(0)], zc_s.at[k - 1], zc_r.at[k - 1], zpeer(k)))
    def metric_send(k):
        for h, (buf, me, to) in enumerate(quarters):
            for m in range(4):
                part = buf.at[c, me[0], m]
                copy(metric_part(h, k, m), part, ms_s.at[h, k - 1], ms_r.at[h, k - 1], to(k)).start()
            part = buf.at[c, me[0]]
            pending.append(copy(part, part, ms_s.at[h, k - 1], ms_r.at[h, k - 1], to(k)))

    metric_send(1)
    metric_send(3)
    fill_tables(sbv, suv, bov, tabv)
    own_tab = pltpu.make_async_copy(tabv, stab.at[0], tab_sem.at[0])
    own_tab.start()
    tab_send = start(copy(tabv, tabr, ex_s.at[0], ex_r.at[0], sibling))
    own_tab.wait()

    zr = zs

    def entry(r, b):
        return stab[0, POS + zr[r], b]

    def half_transform(t, st):
        own = cown[entry(0, stab[0, MU, t])]
        rhs = jnp.concatenate([iv[t, a] for a in range(AB)], axis=1)
        res = jnp.dot(own, rhs, preferred_element_type=F32)
        for a in range(AB):
            bst[st, pl.ds(a, ORB, stride=AB), :] = res[:, a * SH : (a + 1) * SH]
        bp[t] = bst[st].astype(BF16)

    def half_loads(lo, hi):
        @pl.loop(lo, hi)
        def _(i):
            load(i).wait()
            for u in range(PER_LOAD):
                half_transform(i * PER_LOAD + u, u)

    def zwait(r):
        got = spot(r).at[piece(0)]
        copy(got, got, zc_s.at[NZ - r - 1], zc_r.at[NZ - r - 1], sibling).wait_recv()

    def spread(b):
        part = batch(b, piece(0))
        for k in (2, 1, 3):
            start(copy(part, part, xc_s.at[k - 1, b], xc_r.at[k - 1, b], qpeer(k)))
        start(copy(part, part, cc_s.at[0, b], cc_r.at[0, b], sibling))

    def relay(k, b):
        part = batch(b, piece(k))
        copy(part, part, xc_s.at[k - 1, b], xc_r.at[k - 1, b], sibling).wait_recv()
        start(copy(part, part, cc_s.at[k, b], cc_r.at[k, b], sibling))

    half_loads(0, LOADS // 2)
    zwait(7)
    spread(1)
    zwait(1)
    zwait(2)
    spread(0)
    metric_send(2)
    half_loads(LOADS // 2, LOADS)

    rows_c = pl.ds(pl.multiple_of(c * 64, 64), 64)
    rows_n = pl.ds(pl.multiple_of((1 - c) * 64, 64), 64)

    @pl.loop(0, NT, unroll=4)
    def _(k):
        bsend[k] = bp[stab[0, ORDER, k], rows_n, :]

    b_send = start(copy(bsend, bps.at[1], ex_s.at[1], ex_r.at[1], sibling))

    @pl.loop(0, NT, unroll=4)
    def _(k):
        bps[0, k] = bp[stab[0, ORDER, k], rows_c, :]

    for r in (6, 3, 5, 4):
        zwait(r)
    spread(2)

    def got_panel(b):
        for k in (0, 1, 3, 2):
            part = batch(b, piece_n(k))
            copy(part, part, cc_s.at[k, b], cc_r.at[k, b], sibling).wait_recv()

    def transpose_quarters(cc):
        @pl.loop(0, 4)
        def _(i):
            for j in range(4):
                natt[cc, j, i] = nat[cc, i, j].T
                trat[cc, j, i] = tra[cc, i, j].T

    tab_send.wait_recv()
    sib_tab = pltpu.make_async_copy(tabr, stab.at[1], tab_sem.at[1])
    sib_tab.start()
    sib_tab.wait()
    for b in (1, 0):
        for k in (1, 3, 2):
            relay(k, b)
    for b in (1, 0):
        got_panel(b)

    def pick(flag, value):
        return jnp.where(jnp.full(value.shape, flag, I32) == 1, value, 0.0)

    def panel(b, groups):
        return jnp.concatenate([calls[g][i, entry(GROUPS[g][i], b)] for g in groups for i in range(4)], axis=0)

    nt = (((1,), (1,)), ((), ()))

    def m_rows(s):
        base = (c if s == 0 else 1 - c) * 128
        return pl.ds(pl.multiple_of(base, 128), 128)

    def m_part(h, me, j, s):
        return (mg0, mg1)[h].at[me, pl.ds(2 * j, 2), m_rows(s)]

    def ring(h):
        return (ys, ypeer) if h == 0 else (xs, xpeer)

    def m_copy(h, k, j, s):
        me, to = ring(h)
        part = m_part(h, me[0], j, s)
        return copy(part, part, mg_s.at[h, k - 1, j, s], mg_r.at[h, k - 1, j, s], to(k))

    def m_wait(h, j, ks):
        me, to = ring(h)
        for s in range(NC):
            for k in ks:
                part = m_part(h, me[4 - k], j, s)
                copy(part, part, mg_s.at[h, k - 1, j, s], mg_r.at[h, k - 1, j, s], sibling).wait_recv()

    def m_send(j, s):
        for k in (2, 1, 3):
            for h in range(2):
                start(m_copy(h, k, j, s))

    def m_terms(g, s):
        rbuf[s, 0] = jnp.zeros((32, SH), F32)

        @pl.loop(0, NT, unroll=8)
        def _(k):
            part = panel(stab[s, NUS, k], (g,))
            term = lax.dot_general(bps[s, k], part, nt, preferred_element_type=F32)
            term = jnp.concatenate([term[:32], term[32:]], axis=1)
            rbuf[s, k + 1] = term + pick(stab[s, KEEP, k], rbuf[s, k])

        for h in range(NQ // 2):
            got = []
            for u in range(2):
                blk = rbuf[s, stab[s, LAST, 2 * h + u] + 1]
                got.append(pick(stab[s, FILLED, 2 * h + u], blk).reshape(4, AB, SH))
            both = jnp.concatenate(got, axis=1).astype(BF16)
            rows = pl.ds(pl.multiple_of((c if s == 0 else 1 - c) * 128 + h * 16, 16), 16)
            mg0[y, 2 * g : 2 * g + 2, rows, :] = both[:2]
            mg1[x, 2 * g : 2 * g + 2, rows, :] = both[2:]
        m_send(g, s)

    m_terms(0, 0)
    for k in (1, 3, 2):
        relay(k, 2)
    b_send.wait_recv()
    m_terms(0, 1)
    got_panel(2)

    def full_blocks(lo, hi):
        @pl.loop(lo, hi)
        def _(t):
            rhs = iv[t].reshape(AB * SH, SH)
            blk = lax.dot_general(panel(stab[0, NU, t], (0, 1)), rhs, nt, preferred_element_type=F32).astype(BF16)
            for a in range(AB):
                bfull[t, pl.ds(a * SH, SH), :] = blk[:, a * SH : (a + 1) * SH]

    def fit(h, j, near):
        got, me = (mg0, mg1)[h], (ys, xs)[h]
        blocks = [me[k] for k in ((0, 1, 3) if near else (2,))]
        rhs = [jnp.concatenate([got[m, 2 * j], got[m, 2 * j + 1]], axis=1) for m in blocks]
        same, cross = ((natt, tra), (nat, trat))[h]
        lhs = [
            [(same if cr == ck else cross)[(cr, ck)[h], r, m] for m in blocks for ck in range(NC)]
            for r in range(4)
            for cr in range(NC)
        ]
        lhs = jnp.concatenate([jnp.concatenate(v, axis=1) for v in lhs], axis=0)
        res = jnp.dot(lhs, jnp.concatenate(rhs, axis=0), preferred_element_type=F32)
        for r in range(4):
            for u in range(2):
                part = res[r * 256 : (r + 1) * 256, u * SH : (u + 1) * SH]
                fo[h, j, r, u] = part if near else fo[h, j, r, u] + part

    def f_part(h, j, off):
        return fo.at[h, j, (xs, ys)[h][off]]

    def f_copy(h, j, k, cc):
        src = fsend.at[h, j, k - 1, :, pl.ds(cc * 128, 128)]
        to = dev(y, xs[k], cc, z) if h == 0 else dev(ys[k], x, cc, z)
        return copy(src, fgot.at[c, k - 1, h, j], fa_s.at[h, j, k - 1, cc], fa_r.at[h, j, k - 1, c], to)

    def fx(h, j):
        return copy(fxs.at[h, j], fxr.at[h, j], fx_s.at[h, j], fx_r.at[h, j], sibling)

    own_rows = pl.ds(pl.multiple_of(c * 128, 128), 128)
    sib_rows = pl.ds(pl.multiple_of((1 - c) * 128, 128), 128)

    def fits(j):
        for h in range(2):
            m_wait(h, j, (1, 3))
            fit(h, j, True)
        for h in range(2):
            m_wait(h, j, (2,))
            fit(h, j, False)
            for k in (2, 1, 3):
                fsend[h, j, k - 1] = f_part(h, j, k)[...].astype(BF16)
                for cc in range(NC):
                    start(f_copy(h, j, k, cc))
            fxs[h, j] = f_part(h, j, 0)[:, sib_rows].astype(BF16)
            start(fx(h, j))

    def got_from(cs, h, j, u):
        total = f_part(h, j, 0)[u, own_rows] if cs is c else fxr[h, j, u].astype(F32)
        for k in range(3):
            total = total + fgot[cs, k, h, j, u].astype(F32)
        return total

    def totals(j):
        left = lax.broadcasted_iota(I32, (128, SH), 1) < 64
        for h in range(2):
            fx(h, j).wait_recv()
            for k in (1, 3, 2):
                for cc in range(NC):
                    part = fgot.at[cc, k - 1, h, j]
                    copy(part, part, fa_s.at[h, j, k - 1, cc], fa_r.at[h, j, k - 1, cc], sibling).wait_recv()
            for u in range(2):
                for w, cs in enumerate((c, 1 - c)):
                    val = got_from(cs, h, j, u)
                    if j == 0:
                        ta[w, 2 * h + u] = val
                    else:
                        old = ta[w, 2 * h + u]
                        row = JL * w + 2 * h + u
                        ft[pl.ds(row, 128, stride=ORB), :] = jnp.where(left, old, pltpu.roll(val, 64, axis=1))
                        ft[pl.ds(row + 4, 128, stride=ORB), :] = jnp.where(left, pltpu.roll(old, 64, axis=1), val)

    m_terms(1, 0)
    m_terms(1, 1)
    mfs = []
    for h, (buf, me, to) in enumerate(quarters):
        pltpu.make_async_copy(buf.at[c, me[0]], buf.at[c, me[0]], in_sem.at[4 + h]).wait()
        for k in (1, 3, 2):
            part = buf.at[c, me[4 - k]]
            copy(part, part, ms_s.at[h, k - 1], ms_r.at[h, k - 1], sibling).wait_recv()
        mfs.append(start(copy(buf.at[c], buf.at[c], mf_s.at[h], mf_r.at[h], sibling)))

    full_blocks(0, 4)
    transpose_quarters(c)
    for cp in mfs:
        cp.wait_recv()
    transpose_quarters(1 - c)
    full_blocks(4, 10)
    marks = [len(pending)]
    fits(0)
    full_blocks(10, 24)
    fits(1)
    drain(0, marks[0])
    full_blocks(24, NT)
    totals(0)
    totals(1)

    ftq = ft.reshape(NQ, AB * ORB, SH)
    low = pl.ds(pl.multiple_of(c * JL, JL), JL)
    high = pl.ds(pl.multiple_of((1 - c) * JL, JL), JL)

    @pl.loop(0, NT, unroll=16)
    def _(t):
        rows = ftq[stab[0, QQ, t]]
        lhs = jnp.concatenate([rows[a * ORB : (a + 1) * ORB] for a in range(AB)], axis=1)
        res = jnp.dot(lhs.astype(BF16), bfull[t], preferred_element_type=F32)
        gt[t, low, :] = res[:JL]
        gt[t, high, :] = res[JL:]

    for s in range(32):
        one = pick(stab[0, V0, s], gt[stab[0, T0, s]])
        two = pick(stab[0, V1, s], gt[stab[0, T1, s]])
        gs[s % 2, s // 2] = one + two

    g_send = start(copy(gs.at[1 - c], gr, ex_s.at[4], ex_r.at[4], sibling))
    g_send.wait_recv()
    gx[...] = gs[c] + gr[...]
    marks.append(len(pending))
    for k in (10, 6, 14, 9, 11, 5, 7, 13, 15, 2, 8, 1, 3, 4, 12):
        yy, xx = plane(k)
        start(copy(gx.at[yy * NX + xx], gin.at[k], gx_s.at[k - 1], gx_r.at[k - 1], dev(yy, xx, c, z)))
    drain(marks[0], marks[1])
    total = gx[y * NX + x]
    for k in (1, 3, 4, 12, 2, 8, 5, 7, 13, 15, 6, 14, 9, 11, 10):
        copy(gx.at[0], gin.at[k], gx_s.at[k - 1], gx_r.at[k - 1], sibling).wait_recv()
        total = total + gin[k]
    marks.append(len(pending))
    zall[z] = total
    for k in (4, 3, 5, 2, 6, 1, 7):
        start(copy(zall.at[z], zall.at[z], z_s.at[k - 1], z_r.at[k - 1], zpeer(k)))
    drain(marks[1], marks[2])
    for k in (1, 7, 2, 6, 3, 5, 4):
        got = zall.at[zs[NZ - k]]
        copy(got, got, z_s.at[k - 1], z_r.at[k - 1], zpeer(k)).wait_recv()
    whole = zall[...].reshape(NZ * ORB, SH).T
    even = lax.rem(lax.broadcasted_iota(I32, whole.shape, 0), 2) == 0
    out[0] = jnp.where(even, whole, 0.0)
    out[1] = jnp.where(even, 0.0, whole)

    drain(marks[2], len(pending))


def body(integrals, screened_blocks, coeff, support, metric, block_order):
    vm = pltpu.VMEM
    dma = pltpu.SemaphoreType.DMA
    any_spec = pl.BlockSpec(memory_space=pl.ANY)
    res = pl.pallas_call(
        kernel,
        out_shape=jax.ShapeDtypeStruct((2, SH, NZ * ORB), F32),
        in_specs=[any_spec] * 6,
        out_specs=pl.BlockSpec(memory_space=pltpu.VMEM),
        scratch_shapes=[
            vm((ORB, NSUP, SH), BF16),
            vm((3, NT), I32),
            vm((NZ, NSUP), I32),
            vm((1, 32), I32),
            vm((24, 128), I32),
            vm((24, 128), I32),
            pltpu.SMEM((2, 24, 128), I32),
            vm((NT, AB, SH, SH), BF16),
            vm((NZ // 2, NSUP + 1, ORB, SH), BF16),
            vm((NZ // 2, NSUP + 1, ORB, SH), BF16),
            vm((NSUP + 1, ORB, SH), BF16),
            vm((NSUP * ORB, SH), F32),
            vm((PER_LOAD, 128, SH), F32),
            vm((NT, 128, SH), BF16),
            vm((NT, 64, SH), BF16),
            vm((NC, NT, 64, SH), BF16),
            vm((NC, NT + 1, 32, SH), F32),
            vm((NC, 4, 4, 128, 128), BF16),
            vm((NC, 4, 4, 128, 128), BF16),
            vm((NC, 4, 4, 128, 128), BF16),
            vm((NC, 4, 4, 128, 128), BF16),
            vm((4, 4, 256, SH), BF16),
            vm((4, 4, 256, SH), BF16),
            vm((2, 2, 4, 2, 256, SH), F32),
            vm((2, 2, 3, 2, 256, SH), BF16),
            vm((NC, 3, 2, 2, 2, 128, SH), BF16),
            vm((2, 2, 2, 128, SH), BF16),
            vm((2, 2, 2, 128, SH), BF16),
            vm((2, 4, 128, SH), F32),
            vm((128 * ORB, SH), F32),
            vm((NT, AB * SH, SH), BF16),
            vm((NT, ORB, SH), F32),
            vm((NC, 16, ORB, SH), F32),
            vm((16, ORB, SH), F32),
            vm((16, ORB, SH), F32),
            vm((16, ORB, SH), F32),
            vm((NZ, ORB, SH), F32),
            dma((6,)), dma((LOADS,)), dma((2,)),
            dma((7,)), dma((7,)), dma((3, 3)), dma((3, 3)), dma((4, 3)), dma((4, 3)),
            dma((2, 3)), dma((2, 3)), dma((2,)), dma((2,)),
            dma((5,)), dma((5,)),
            dma((2, 3, 2, 2)), dma((2, 3, 2, 2)), dma((2, 2, 3, 2)), dma((2, 2, 3, 2)), dma((2, 2)), dma((2, 2)),
            dma((15,)), dma((15,)), dma((7,)), dma((7,)),
        ],
        compiler_params=pltpu.CompilerParams(
            collective_id=0, has_side_effects=True, vmem_limit_bytes=56 * 1024 * 1024
        ),
        cost_estimate=pl.CostEstimate(flops=4 * 10**9, bytes_accessed=10 * 10**6, transcendentals=0),
        name="exchange",
    )(integrals, coeff, metric, screened_blocks.T, support, block_order.reshape(1, -1))
    return (res[0] + res[1])[None]


def solution(mesh):
    in_specs = (
        P("aux", None, None, None),
        P("aux", None),
        P("occ", None, None),
        P(),
        P("aux", None),
        P(),
    )
    return jax.shard_map(
        body, mesh=mesh, in_specs=in_specs, out_specs=P("aux", None, None), check_vma=False
    )
```

```python
import jax
import jax.numpy as jnp
from jax import lax
from jax.experimental import pallas as pl
from jax.experimental.pallas import tpu as pltpu
from jax.sharding import PartitionSpec as P

MESH = pl.DeviceIdType.MESH
F32 = jnp.float32
BF16 = jnp.bfloat16
I32 = jnp.int32
NY, NX, NC, NZ = 4, 4, 2, 8
NT, AB, SH, ORB, NSUP, NQ = 32, 8, 128, 16, 24, 16
JL = ORB // NC
PIECE = NSUP // (NX * NC)
LOADS = 8
PER_LOAD = NT // LOADS
ORDER, KEEP, NUS, MU, NU, LAST, FILLED, QQ, T0, T1, V0, V1, POS = 0, 1, 2, 3, 4, 5, 6, 7, 8, 9, 10, 11, 16
BATCHES = ((0, 1, 2), (0, 3, 1), (1, 0, 4))
GROUPS = ((0, 1, 2, 7), (3, 4, 5, 6))


def fill_tables(sbv, suv, bov, tabv):
    t = lax.broadcasted_iota(I32, (NT, NT), 0)
    lane = lax.broadcasted_iota(I32, (NT, NT), 1)

    def down(mask, value):
        return jnp.sum(jnp.where(mask, value, 0), axis=0, keepdims=True)

    def across(mask, value=1):
        return jnp.sum(jnp.where(mask, value, 0), axis=1, keepdims=True)

    diagonal, before = t == lane, lane < t
    mu_r, nu_r, q_r = [sbv[i : i + 1, :] for i in range(3)]
    mu, nu, q = [across(diagonal, v) for v in (mu_r, nu_r, q_r)]
    rank = across((q_r < q) | ((q_r == q) & before))
    follows = across((q_r == q) & before)
    second = across((mu_r == mu) & before)
    placed = rank == lane
    here = bov[...] == mu
    one, two = here & (second == 0), here & (second > 0)
    rows = {
        ORDER: down(placed, t),
        KEEP: down(placed & (follows > 0), 1),
        NUS: down(placed, jnp.broadcast_to(nu, (NT, NT))),
        MU: mu_r,
        NU: nu_r,
        LAST: jnp.maximum(down(q <= lane, 1) - 1, 0),
        FILLED: jnp.minimum(down(q == lane, 1), 1),
        QQ: q_r,
        T0: jnp.max(jnp.where(one, t, 0), axis=0, keepdims=True),
        T1: jnp.max(jnp.where(two, t, 0), axis=0, keepdims=True),
        V0: down(one, 1),
        V1: down(two, 1),
    }
    for i, v in rows.items():
        tabv[i : i + 1, 0:NT] = v
    block = lax.broadcasted_iota(I32, (NZ, 32), 1)
    pos = jnp.full((NZ, 32), NSUP, I32)
    for s in range(NSUP):
        pos = jnp.where(jnp.broadcast_to(suv[:, s : s + 1], (NZ, 32)) == block, s, pos)
    tabv[POS : POS + NZ, 0:32] = pos


def kernel(
    ints, coeff, metric, sb, support, border, out,
    cin, sbv, suv, bov, tabv, tabr, stab,
    iv, calla, callb, cown, c32, bst, bp, bsend, bps, rbuf, nat, tra, natt, trat, mg0, mg1, fo, fsend, fgot,
    fxs, fxr, ta, ft, bfull, gt, gs, gr, gx, gin, zall,
    in_sem, int_sem, tab_sem, zc_s, zc_r, xc_s, xc_r, cc_s, cc_r, ms_s, ms_r, mf_s, mf_r,
    ex_s, ex_r, mg_s, mg_r, fa_s, fa_r, fx_s, fx_r, gx_s, gx_r, z_s, z_r,
):
    d = lax.axis_index("aux")
    z = lax.axis_index("occ")
    y, x, c = d // (NX * NC), (d // NC) % NX, d % NC
    ys, xs, zs = [[lax.rem(v + k, n) for k in range(n)] for v, n in ((y, NY), (x, NX), (z, NZ))]

    def dev(yy, xx, cc, zz):
        return (yy * (NX * NC) + xx * NC + cc, zz)

    sibling = dev(y, x, 1 - c, z)

    def zpeer(k):
        return dev(y, x, c, zs[k])

    def xpeer(k):
        return dev(y, xs[k], c, z)

    def ypeer(k):
        return dev(ys[k], x, c, z)

    def plane(k):
        return ys[k // NX], xs[k % NX]

    def copy(src, dst, s, r, to):
        return pltpu.make_async_remote_copy(
            src_ref=src, dst_ref=dst, send_sem=s, recv_sem=r, device_id=to, device_id_type=MESH
        )

    pending = []

    def start(cp):
        cp.start()
        pending.append(cp)
        return cp

    def drain(lo, hi):
        for cp in pending[lo:hi]:
            cp.wait_send()

    def load(i):
        part = pl.ds(i * PER_LOAD, PER_LOAD)
        return pltpu.make_async_copy(ints.at[part], iv.at[part], int_sem.at[i])

    small = [
        pltpu.make_async_copy(src, dst, in_sem.at[i])
        for i, (src, dst) in enumerate(((coeff, cin), (sb, sbv), (support, suv), (border, bov)))
    ]
    for cp in small:
        cp.start()
    barrier = pltpu.get_barrier_semaphore()
    partners = [zpeer(k) for k in (4, 3, 5, 2, 6, 1, 7)]
    partners += [dev(*plane(k), c, z) for k in range(1, NX * NY)]
    partners += [sibling]
    partners += [dev(y, xs[k], 1 - c, z) for k in (1, 2, 3)]
    partners += [dev(ys[k], x, 1 - c, z) for k in (1, 2, 3)]
    for who in partners:
        pl.semaphore_signal(barrier, inc=1, device_id=who, device_id_type=MESH)
    for i in range(LOADS):
        load(i).start()

    def metric_part(h, k, m):
        if h == 0:
            col = (ys[k] * NX + m) * 256 + c * 128
        else:
            col = (m * NX + xs[k]) * 256 + (1 - c) * 128
        return metric.at[:, pl.ds(pl.multiple_of(col, 128), 128)]

    quarters = ((nat, ys, ypeer), (tra, xs, xpeer))
    for h, (buf, me, to) in enumerate(quarters):
        for m in range(4):
            pltpu.make_async_copy(metric_part(h, 0, m), buf.at[c, me[0], m], in_sem.at[4 + h]).start()

    small[0].wait()
    for i in range(ORB):
        c32[pl.ds(i, NSUP, stride=ORB), :] = cin[i].astype(F32)
    cown[:NSUP] = c32[...].astype(BF16).reshape(NSUP, ORB, SH)
    cown[NSUP] = jnp.zeros((ORB, SH), BF16)
    calla[0] = cown[...]
    for k in range(NZ // 2):
        calla[k, NSUP] = jnp.zeros((ORB, SH), BF16)
        callb[k, NSUP] = jnp.zeros((ORB, SH), BF16)
    tabv[...] = jnp.zeros(tabv.shape, I32)
    for cp in small[1:]:
        cp.wait()

    pl.semaphore_wait(barrier, len(partners))

    place = [xs[k] * (1 - c) + ys[k] * c for k in range(4)]
    place_n = [xs[k] * c + ys[k] * (1 - c) for k in range(4)]

    calls = (calla, callb)

    def spot(r):
        g = int(r in GROUPS[1])
        return calls[g].at[GROUPS[g].index(r)]

    def batch(b, part):
        g, lo, n = BATCHES[b]
        return calls[g].at[pl.ds(lo, n), part]

    def piece(k):
        return pl.ds(c * (NSUP // NC) + PIECE * place[(4 - k) % 4], PIECE)

    def piece_n(k):
        return pl.ds((1 - c) * (NSUP // NC) + PIECE * place_n[(4 - k) % 4], PIECE)

    def qpeer(k):
        return dev(ys[k] * c + y * (1 - c), xs[k] * (1 - c) + x * c, c, z)

    for k in (7, 1, 6, 4, 3, 5, 2):
        start(copy(cown.at[piece(0)], spot(NZ - k).at[piece(0)], zc_s.at[k - 1], zc_r.at[k - 1], zpeer(k)))
    def metric_send(k):
        for h, (buf, me, to) in enumerate(quarters):
            for m in range(4):
                part = buf.at[c, me[0], m]
                copy(metric_part(h, k, m), part, ms_s.at[h, k - 1], ms_r.at[h, k - 1], to(k)).start()
            part = buf.at[c, me[0]]
            pending.append(copy(part, part, ms_s.at[h, k - 1], ms_r.at[h, k - 1], to(k)))

    metric_send(1)
    metric_send(3)
    fill_tables(sbv, suv, bov, tabv)
    own_tab = pltpu.make_async_copy(tabv, stab.at[0], tab_sem.at[0])
    own_tab.start()
    tab_send = start(copy(tabv, tabr, ex_s.at[0], ex_r.at[0], sibling))
    own_tab.wait()

    zr = zs

    def entry(r, b):
        return stab[0, POS + zr[r], b]

    def half_transform(t, st):
        own = cown[entry(0, stab[0, MU, t])]
        rhs = jnp.concatenate([iv[t, a] for a in range(AB)], axis=1)
        res = jnp.dot(own, rhs, preferred_element_type=F32)
        for a in range(AB):
            bst[st, pl.ds(a, ORB, stride=AB), :] = res[:, a * SH : (a + 1) * SH]
        bp[t] = bst[st].astype(BF16)

    def half_loads(lo, hi):
        @pl.loop(lo, hi)
        def _(i):
            load(i).wait()
            for u in range(PER_LOAD):
                half_transform(i * PER_LOAD + u, u)

    def zwait(r):
        got = spot(r).at[piece(0)]
        copy(got, got, zc_s.at[NZ - r - 1], zc_r.at[NZ - r - 1], sibling).wait_recv()

    def spread(b):
        part = batch(b, piece(0))
        for k in (2, 1, 3):
            start(copy(part, part, xc_s.at[k - 1, b], xc_r.at[k - 1, b], qpeer(k)))
        start(copy(part, part, cc_s.at[0, b], cc_r.at[0, b], sibling))

    def relay(k, b):
        part = batch(b, piece(k))
        copy(part, part, xc_s.at[k - 1, b], xc_r.at[k - 1, b], sibling).wait_recv()
        start(copy(part, part, cc_s.at[k, b], cc_r.at[k, b], sibling))

    half_loads(0, LOADS // 2)
    zwait(7)
    spread(1)
    zwait(1)
    zwait(2)
    spread(0)
    metric_send(2)
    half_loads(LOADS // 2, LOADS)

    rows_c = pl.ds(pl.multiple_of(c * 64, 64), 64)
    rows_n = pl.ds(pl.multiple_of((1 - c) * 64, 64), 64)

    @pl.loop(0, NT, unroll=4)
    def _(k):
        bsend[k] = bp[stab[0, ORDER, k], rows_n, :]

    b_send = start(copy(bsend, bps.at[1], ex_s.at[1], ex_r.at[1], sibling))

    @pl.loop(0, NT, unroll=4)
    def _(k):
        bps[0, k] = bp[stab[0, ORDER, k], rows_c, :]

    for r in (6, 3, 5, 4):
        zwait(r)
    spread(2)

    def got_panel(b):
        for k in (0, 1, 3, 2):
            part = batch(b, piece_n(k))
            copy(part, part, cc_s.at[k, b], cc_r.at[k, b], sibling).wait_recv()

    def transpose_quarters(cc):
        @pl.loop(0, 4)
        def _(i):
            for j in range(4):
                natt[cc, j, i] = nat[cc, i, j].T
                trat[cc, j, i] = tra[cc, i, j].T

    tab_send.wait_recv()
    sib_tab = pltpu.make_async_copy(tabr, stab.at[1], tab_sem.at[1])
    sib_tab.start()
    sib_tab.wait()
    for b in (1, 0):
        for k in (1, 3, 2):
            relay(k, b)
    for b in (1, 0):
        got_panel(b)

    def pick(flag, value):
        return jnp.where(jnp.full(value.shape, flag, I32) == 1, value, 0.0)

    def panel(b, groups):
        return jnp.concatenate([calls[g][i, entry(GROUPS[g][i], b)] for g in groups for i in range(4)], axis=0)

    nt = (((1,), (1,)), ((), ()))

    def m_rows(s):
        base = (c if s == 0 else 1 - c) * 128
        return pl.ds(pl.multiple_of(base, 128), 128)

    def m_part(h, me, j, s):
        return (mg0, mg1)[h].at[me, pl.ds(2 * j, 2), m_rows(s)]

    def ring(h):
        return (ys, ypeer) if h == 0 else (xs, xpeer)

    def m_copy(h, k, j, s):
        me, to = ring(h)
        part = m_part(h, me[0], j, s)
        return copy(part, part, mg_s.at[h, k - 1, j, s], mg_r.at[h, k - 1, j, s], to(k))

    def m_wait(h, j, ks):
        me, to = ring(h)
        for s in range(NC):
            for k in ks:
                part = m_part(h, me[4 - k], j, s)
                copy(part, part, mg_s.at[h, k - 1, j, s], mg_r.at[h, k - 1, j, s], sibling).wait_recv()

    def m_send(j, s):
        for k in (2, 1, 3):
            for h in range(2):
                start(m_copy(h, k, j, s))

    def m_terms(g, s):
        rbuf[s, 0] = jnp.zeros((32, SH), F32)

        @pl.loop(0, NT, unroll=16)
        def _(k):
            part = panel(stab[s, NUS, k], (g,))
            term = lax.dot_general(bps[s, k], part, nt, preferred_element_type=F32)
            term = jnp.concatenate([term[:32], term[32:]], axis=1)
            rbuf[s, k + 1] = term + pick(stab[s, KEEP, k], rbuf[s, k])

        for h in range(NQ // 2):
            got = []
            for u in range(2):
                blk = rbuf[s, stab[s, LAST, 2 * h + u] + 1]
                got.append(pick(stab[s, FILLED, 2 * h + u], blk).reshape(4, AB, SH))
            both = jnp.concatenate(got, axis=1).astype(BF16)
            rows = pl.ds(pl.multiple_of((c if s == 0 else 1 - c) * 128 + h * 16, 16), 16)
            mg0[y, 2 * g : 2 * g + 2, rows, :] = both[:2]
            mg1[x, 2 * g : 2 * g + 2, rows, :] = both[2:]
        m_send(g, s)

    m_terms(0, 0)
    for k in (1, 3, 2):
        relay(k, 2)
    b_send.wait_recv()
    m_terms(0, 1)
    got_panel(2)

    def full_blocks(lo, hi):
        @pl.loop(lo, hi)
        def _(t):
            rhs = iv[t].reshape(AB * SH, SH)
            blk = lax.dot_general(panel(stab[0, NU, t], (0, 1)), rhs, nt, preferred_element_type=F32).astype(BF16)
            for a in range(AB):
                bfull[t, pl.ds(a * SH, SH), :] = blk[:, a * SH : (a + 1) * SH]

    def fit(h, j, near):
        got, me = (mg0, mg1)[h], (ys, xs)[h]
        blocks = [me[k] for k in ((0, 1, 3) if near else (2,))]
        rhs = [jnp.concatenate([got[m, 2 * j], got[m, 2 * j + 1]], axis=1) for m in blocks]
        same, cross = ((natt, tra), (nat, trat))[h]
        lhs = [
            [(same if cr == ck else cross)[(cr, ck)[h], r, m] for m in blocks for ck in range(NC)]
            for r in range(4)
            for cr in range(NC)
        ]
        lhs = jnp.concatenate([jnp.concatenate(v, axis=1) for v in lhs], axis=0)
        res = jnp.dot(lhs, jnp.concatenate(rhs, axis=0), preferred_element_type=F32)
        for r in range(4):
            for u in range(2):
                part = res[r * 256 : (r + 1) * 256, u * SH : (u + 1) * SH]
                fo[h, j, r, u] = part if near else fo[h, j, r, u] + part

    def f_part(h, j, off):
        return fo.at[h, j, (xs, ys)[h][off]]

    def f_copy(h, j, k, cc):
        src = fsend.at[h, j, k - 1, :, pl.ds(cc * 128, 128)]
        to = dev(y, xs[k], cc, z) if h == 0 else dev(ys[k], x, cc, z)
        return copy(src, fgot.at[c, k - 1, h, j], fa_s.at[h, j, k - 1, cc], fa_r.at[h, j, k - 1, c], to)

    def fx(h, j):
        return copy(fxs.at[h, j], fxr.at[h, j], fx_s.at[h, j], fx_r.at[h, j], sibling)

    own_rows = pl.ds(pl.multiple_of(c * 128, 128), 128)
    sib_rows = pl.ds(pl.multiple_of((1 - c) * 128, 128), 128)

    def fits(j):
        for h in range(2):
            m_wait(h, j, (1, 3))
            fit(h, j, True)
        for h in range(2):
            m_wait(h, j, (2,))
            fit(h, j, False)
            for k in (2, 1, 3):
                fsend[h, j, k - 1] = f_part(h, j, k)[...].astype(BF16)
                for cc in range(NC):
                    start(f_copy(h, j, k, cc))
            fxs[h, j] = f_part(h, j, 0)[:, sib_rows].astype(BF16)
            start(fx(h, j))

    def got_from(cs, h, j, u):
        total = f_part(h, j, 0)[u, own_rows] if cs is c else fxr[h, j, u].astype(F32)
        for k in range(3):
            total = total + fgot[cs, k, h, j, u].astype(F32)
        return total

    def totals(j):
        left = lax.broadcasted_iota(I32, (128, SH), 1) < 64
        for h in range(2):
            fx(h, j).wait_recv()
            for k in (1, 3, 2):
                for cc in range(NC):
                    part = fgot.at[cc, k - 1, h, j]
                    copy(part, part, fa_s.at[h, j, k - 1, cc], fa_r.at[h, j, k - 1, cc], sibling).wait_recv()
            for u in range(2):
                for w, cs in enumerate((c, 1 - c)):
                    val = got_from(cs, h, j, u)
                    if j == 0:
                        ta[w, 2 * h + u] = val
                    else:
                        old = ta[w, 2 * h + u]
                        row = JL * w + 2 * h + u
                        ft[pl.ds(row, 128, stride=ORB), :] = jnp.where(left, old, pltpu.roll(val, 64, axis=1))
                        ft[pl.ds(row + 4, 128, stride=ORB), :] = jnp.where(left, pltpu.roll(old, 64, axis=1), val)

    m_terms(1, 0)
    m_terms(1, 1)
    mfs = []
    for h, (buf, me, to) in enumerate(quarters):
        pltpu.make_async_copy(buf.at[c, me[0]], buf.at[c, me[0]], in_sem.at[4 + h]).wait()
        for k in (1, 3, 2):
            part = buf.at[c, me[4 - k]]
            copy(part, part, ms_s.at[h, k - 1], ms_r.at[h, k - 1], sibling).wait_recv()
        mfs.append(start(copy(buf.at[c], buf.at[c], mf_s.at[h], mf_r.at[h], sibling)))

    full_blocks(0, 4)
    transpose_quarters(c)
    for cp in mfs:
        cp.wait_recv()
    transpose_quarters(1 - c)
    full_blocks(4, 10)
    marks = [len(pending)]
    fits(0)
    full_blocks(10, 24)
    fits(1)
    drain(0, marks[0])
    full_blocks(24, NT)
    totals(0)
    totals(1)

    ftq = ft.reshape(NQ, AB * ORB, SH)
    low = pl.ds(pl.multiple_of(c * JL, JL), JL)
    high = pl.ds(pl.multiple_of((1 - c) * JL, JL), JL)

    @pl.loop(0, NT, unroll=16)
    def _(t):
        rows = ftq[stab[0, QQ, t]]
        lhs = jnp.concatenate([rows[a * ORB : (a + 1) * ORB] for a in range(AB)], axis=1)
        res = jnp.dot(lhs.astype(BF16), bfull[t], preferred_element_type=F32)
        gt[t, low, :] = res[:JL]
        gt[t, high, :] = res[JL:]

    for s in range(32):
        one = pick(stab[0, V0, s], gt[stab[0, T0, s]])
        two = pick(stab[0, V1, s], gt[stab[0, T1, s]])
        gs[s % 2, s // 2] = one + two

    g_send = start(copy(gs.at[1 - c], gr, ex_s.at[4], ex_r.at[4], sibling))
    g_send.wait_recv()
    gx[...] = gs[c] + gr[...]
    marks.append(len(pending))
    for k in (10, 6, 14, 9, 11, 5, 7, 13, 15, 2, 8, 1, 3, 4, 12):
        yy, xx = plane(k)
        start(copy(gx.at[yy * NX + xx], gin.at[k], gx_s.at[k - 1], gx_r.at[k - 1], dev(yy, xx, c, z)))
    drain(marks[0], marks[1])
    total = gx[y * NX + x]
    for k in (1, 3, 4, 12, 2, 8, 5, 7, 13, 15, 6, 14, 9, 11, 10):
        copy(gx.at[0], gin.at[k], gx_s.at[k - 1], gx_r.at[k - 1], sibling).wait_recv()
        total = total + gin[k]
    marks.append(len(pending))
    zall[z] = total
    for k in (4, 3, 5, 2, 6, 1, 7):
        start(copy(zall.at[z], zall.at[z], z_s.at[k - 1], z_r.at[k - 1], zpeer(k)))
    drain(marks[1], marks[2])
    for k in (1, 7, 2, 6, 3, 5, 4):
        got = zall.at[zs[NZ - k]]
        copy(got, got, z_s.at[k - 1], z_r.at[k - 1], zpeer(k)).wait_recv()
    out[...] = zall[...].reshape(NZ * ORB, SH).T

    drain(marks[2], len(pending))


def body(integrals, screened_blocks, coeff, support, metric, block_order):
    vm = pltpu.VMEM
    dma = pltpu.SemaphoreType.DMA
    any_spec = pl.BlockSpec(memory_space=pl.ANY)
    res = pl.pallas_call(
        kernel,
        out_shape=jax.ShapeDtypeStruct((SH, NZ * ORB), F32),
        in_specs=[any_spec] * 6,
        out_specs=pl.BlockSpec(memory_space=pltpu.VMEM),
        scratch_shapes=[
            vm((ORB, NSUP, SH), BF16),
            vm((3, NT), I32),
            vm((NZ, NSUP), I32),
            vm((1, 32), I32),
            vm((24, 128), I32),
            vm((24, 128), I32),
            pltpu.SMEM((2, 24, 128), I32),
            vm((NT, AB, SH, SH), BF16),
            vm((NZ // 2, NSUP + 1, ORB, SH), BF16),
            vm((NZ // 2, NSUP + 1, ORB, SH), BF16),
            vm((NSUP + 1, ORB, SH), BF16),
            vm((NSUP * ORB, SH), F32),
            vm((PER_LOAD, 128, SH), F32),
            vm((NT, 128, SH), BF16),
            vm((NT, 64, SH), BF16),
            vm((NC, NT, 64, SH), BF16),
            vm((NC, NT + 1, 32, SH), F32),
            vm((NC, 4, 4, 128, 128), BF16),
            vm((NC, 4, 4, 128, 128), BF16),
            vm((NC, 4, 4, 128, 128), BF16),
            vm((NC, 4, 4, 128, 128), BF16),
            vm((4, 4, 256, SH), BF16),
            vm((4, 4, 256, SH), BF16),
            vm((2, 2, 4, 2, 256, SH), F32),
            vm((2, 2, 3, 2, 256, SH), BF16),
            vm((NC, 3, 2, 2, 2, 128, SH), BF16),
            vm((2, 2, 2, 128, SH), BF16),
            vm((2, 2, 2, 128, SH), BF16),
            vm((2, 4, 128, SH), F32),
            vm((128 * ORB, SH), F32),
            vm((NT, AB * SH, SH), BF16),
            vm((NT, ORB, SH), F32),
            vm((NC, 16, ORB, SH), F32),
            vm((16, ORB, SH), F32),
            vm((16, ORB, SH), F32),
            vm((16, ORB, SH), F32),
            vm((NZ, ORB, SH), F32),
            dma((6,)), dma((LOADS,)), dma((2,)),
            dma((7,)), dma((7,)), dma((3, 3)), dma((3, 3)), dma((4, 3)), dma((4, 3)),
            dma((2, 3)), dma((2, 3)), dma((2,)), dma((2,)),
            dma((5,)), dma((5,)),
            dma((2, 3, 2, 2)), dma((2, 3, 2, 2)), dma((2, 2, 3, 2)), dma((2, 2, 3, 2)), dma((2, 2)), dma((2, 2)),
            dma((15,)), dma((15,)), dma((7,)), dma((7,)),
        ],
        compiler_params=pltpu.CompilerParams(
            collective_id=0, has_side_effects=True, vmem_limit_bytes=56 * 1024 * 1024
        ),
        cost_estimate=pl.CostEstimate(flops=4 * 10**9, bytes_accessed=10 * 10**6, transcendentals=0),
        name="exchange",
    )(integrals, coeff, metric, screened_blocks.T, support, block_order.reshape(1, -1))
    return res[None]


def solution(mesh):
    in_specs = (
        P("aux", None, None, None),
        P("aux", None),
        P("occ", None, None),
        P(),
        P("aux", None),
        P(),
    )
    return jax.shard_map(
        body, mesh=mesh, in_specs=in_specs, out_specs=P("aux", None, None), check_vma=False
    )
```
